128 devices in a mesh: ctx: 32 (over z, x, core), head: 4 (over y).
Axes of the slice: x: 4, y: 4, z: 4, core: 2. Of those that a mesh axis runs over, the one named last changes fastest.
Arguments:
- query: bfloat16 [8, 16384, 256], P(None, ('ctx', 'head')), may hold values from -6 to 6
- keys: bfloat16 [8, 16384, 256], P(None, ('ctx', 'head')), may hold values from -6 to 6
- values: bfloat16 [8, 16384, 512], P(None, ('ctx', 'head')), may hold values from -6 to 6
- igate: bfloat16 [8, 16384], P(None, ('ctx', 'head')), may hold values from -8 to 0
- fgate: bfloat16 [8, 16384], P(None, ('ctx', 'head')), may hold values from 0 to 16
- hidden_output_gradient: bfloat16 [8, 16384, 512], P(None, ('ctx', 'head')), may hold values from -6 to 6
- doc_start: int32 [16384], P('ctx'), may hold values 0 or 1
Outputs:
- hidden_out: bfloat16 [8, 16384, 512], P(None, ('ctx', 'head'))
- grad_query: bfloat16 [8, 16384, 256], P(None, ('ctx', 'head'))
- grad_keys: bfloat16 [8, 16384, 256], P(None, ('ctx', 'head'))
- grad_values: bfloat16 [8, 16384, 512], P(None, ('ctx', 'head'))
- input_gate_gradient: bfloat16 [8, 16384], P(None, ('ctx', 'head'))
- grad_fgate: bfloat16 [8, 16384], P(None, ('ctx', 'head'))
The draws below stay inside these ranges and needn't reach their ends.
Inputs may be any that keep to these rules, and one draw needn't show every extreme that they name: `doc_start`: 1 marks the first token of a document; tokens separated by a document start do not interact.
All inputs are finite; a program needn't handle non-finite values. No bound on the sum of `doc_start` on one device may be relied on, other than what follows from the above.
Results may differ from the reference program's by a relative error of at most 0.038.
Values may be sent and summed in bfloat16 or wider, within the bound.
No kernel may reach another device: no remote copies, remote signals or barrier semaphores. Data moves between devices by JAX's collectives and lax.ppermute only.
A program may use at most 192 MiB of HBM per device.

```python
import jax
import jax.numpy as jnp
from jax import lax

HEAD_COUNT = 8
DQK = 256
DV = 512
TOK_DEV = 128
SEQUENCE_TOKENS = 16384
N_CTX = 32


def gate_fields(key, slow_share):
    key_sequence = jax.random.split(key, 8)
    slow_head = jax.random.uniform(key_sequence[0], (HEAD_COUNT, 1)) < slow_share
    rate_scale = jax.random.uniform(key_sequence[1], (HEAD_COUNT, 1), minval=0.2, maxval=1.0)
    quick_span = jax.random.uniform(key_sequence[2], (HEAD_COUNT, 1), minval=25.0, maxval=50.0)
    window = jnp.where(slow_head, SEQUENCE_TOKENS / rate_scale, quick_span)
    roughness = jax.random.uniform(key_sequence[3], (HEAD_COUNT, SEQUENCE_TOKENS), minval=0.5, maxval=2.0)
    span_count = SEQUENCE_TOKENS // TOK_DEV
    level_factor = jnp.exp(jax.random.uniform(key_sequence[4], (HEAD_COUNT, span_count, 1), minval=-0.7, maxval=0.7))
    level_factor = jnp.broadcast_to(level_factor, (HEAD_COUNT, span_count, TOK_DEV)).reshape(HEAD_COUNT, SEQUENCE_TOKENS)
    leak_rate = roughness * level_factor / window
    forget_gate_values = jnp.log((1.0 - leak_rate) / leak_rate)
    spike_mask = jax.random.uniform(key_sequence[5], (HEAD_COUNT, SEQUENCE_TOKENS)) < 2.0 / SEQUENCE_TOKENS
    spike_value = jax.random.uniform(key_sequence[6], (HEAD_COUNT, SEQUENCE_TOKENS), minval=0.0, maxval=1.4)
    forget_gate_values = jnp.where(spike_mask, spike_value, forget_gate_values)
    ingate = -0.5 * jnp.log(window) - 1.0 + jax.random.uniform(key_sequence[7], (HEAD_COUNT, SEQUENCE_TOKENS), minval=-1.0, maxval=1.0)
    ingate = jnp.clip(ingate, -8.0, 0.0)
    return (ingate.astype(jnp.float32), forget_gate_values.astype(jnp.float32))


def draw_igate(key, part):
    slow_share = 0.5
    ingate, forget_gate_values = gate_fields(key, slow_share)
    return ingate.astype(jnp.bfloat16)


def draw_fgate(key, part):
    slow_share = 0.5
    ingate, forget_gate_values = gate_fields(key, slow_share)
    return forget_gate_values.astype(jnp.bfloat16)


def touch_ends(entries, rng, least, largest):
    shape = entries.shape
    index_at = [jax.random.randint(jax.random.fold_in(rng, axis), (), 0, shape[axis]) for axis in range(len(shape))]
    entries = entries.at[tuple(index_at)].set(least)
    longest = shape.index(max(shape))
    index_at[longest] = (index_at[longest] + 1) % shape[longest]
    return entries.at[tuple(index_at)].set(largest)


def steps_of(rng, dims, shards, low, high):
    level = 1.0
    for dim, shards_of in shards:
        draws = jax.random.uniform(jax.random.fold_in(jax.random.fold_in(rng, 6), dim), (shards_of,), jnp.float32, low / len(shards), high / len(shards))
        level = level * jnp.repeat(jnp.exp(draws), dims[dim] // shards_of).reshape((-1,) + (1,) * (len(dims) - 1 - dim))
    return level


def centred(key, shape, scale, reach, pieces=(), held_as=jnp.bfloat16):
    values = jax.random.normal(key, shape, jnp.float32) * scale
    if len(pieces) > 0:
        values = steps_of(key, shape, pieces, -0.22, 0.18) * values
    return jnp.clip(values, min=-reach, max=reach).astype(held_as)


def setup_inputs(seed: int = 0) -> dict:
    splits = jax.random.split(jax.random.key(seed), 8)
    return {
        "query": centred(splits[0], (HEAD_COUNT, SEQUENCE_TOKENS, DQK), 1.0, 6.0, ((1, 128),)),
        "keys": centred(splits[1], (HEAD_COUNT, SEQUENCE_TOKENS, DQK), 1.0, 6.0, ((1, 128),)),
        "values": centred(splits[2], (HEAD_COUNT, SEQUENCE_TOKENS, DV), 1.0, 6.0, ((1, 128),)),
        "igate": draw_igate(jax.random.fold_in(splits[7], 71), 0),
        "fgate": draw_fgate(jax.random.fold_in(splits[7], 71), 0),
        "hidden_output_gradient": centred(splits[5], (HEAD_COUNT, SEQUENCE_TOKENS, DV), 1.0, 6.0, ((1, 128),)),
        "doc_start": touch_ends((jax.random.randint(splits[6], (SEQUENCE_TOKENS,), 0, TOK_DEV * 32) < 1).astype(jnp.int32), jax.random.fold_in(splits[6], 1), 0, 1),
    }


neg_large = -1e+30
highest = lax.Precision.HIGHEST

def contract(form, left, right):
    return jnp.einsum(form, left.astype(jnp.float32), right.astype(jnp.float32), precision=highest)

def block_local(query, keys, values, igate, fgate, starts):
    length = query.shape[1]
    query_scale = query.shape[2] ** (-0.5)
    log_forget = jax.nn.log_sigmoid(fgate.astype(jnp.float32))
    cumulative = jnp.cumsum(log_forget, axis=1)
    segment = jnp.cumsum(starts.astype(jnp.int32))
    ingate = igate.astype(jnp.float32)
    position = lax.broadcasted_iota(jnp.int32, (length, length), 0)
    source = lax.broadcasted_iota(jnp.int32, (length, length), 1)
    allowed = (position >= source) & (segment[:, None] == segment[None, :])
    log_weight = cumulative[:, :, None] - cumulative[:, None, :] + ingate[:, None, :]
    weight = jnp.exp(jnp.where(allowed[None], log_weight, neg_large))
    scores = contract('htd,hsd->hts', query, keys) * query_scale
    pair_weight = (weight * scores).astype(jnp.bfloat16)
    tail_mask = (segment == segment[length - 1])[None, :]
    alpha_weight = jnp.where(tail_mask, jnp.exp(cumulative[:, length - 1:] - cumulative + ingate), 0.0)
    beta_weight = jnp.where((segment == 0)[None, :], jnp.exp(cumulative), 0.0)
    decay_factor = jnp.where(segment[length - 1] == 0, jnp.exp(cumulative[:, length - 1]), 0.0)
    keys_alpha = (alpha_weight[:, :, None] * keys.astype(jnp.float32)).astype(jnp.bfloat16)
    update = contract('hsd,hsv->hdv', keys_alpha, values)
    update_n = lax.optimization_barrier(jnp.sum(keys_alpha.astype(jnp.float32), axis=1))
    return (weight, pair_weight, alpha_weight, beta_weight, decay_factor, update, update_n)

def block_output(query, values, pair_weight, beta_weight, state_in, state_n_in):
    query_scale = query.shape[2] ** (-0.5)
    state_bf = state_in.astype(jnp.bfloat16)
    state_n_bf = state_n_in.astype(jnp.bfloat16)
    cross = contract('htd,hdv->htv', query, state_bf)
    numerator = contract('hts,hsv->htv', pair_weight, values) + beta_weight[:, :, None] * cross * query_scale
    cross_n = lax.optimization_barrier(jnp.sum(query.astype(jnp.float32) * state_n_bf.astype(jnp.float32)[:, None, :], axis=2))
    denominator = lax.optimization_barrier(jnp.sum(pair_weight.astype(jnp.float32), axis=2)) + beta_weight * cross_n * query_scale
    norm_value = jnp.sqrt(denominator * denominator + 1.0)
    hidden = numerator / norm_value[:, :, None]
    return (hidden, denominator, norm_value, state_bf, state_n_bf)

def block_backward(query, keys, values, hidden_output_gradient, weight, pair_weight, beta_weight, hidden, denominator, norm_value):
    query_scale = query.shape[2] ** (-0.5)
    grad_float = hidden_output_gradient.astype(jnp.float32)
    num_grad = (grad_float / norm_value[:, :, None]).astype(jnp.bfloat16)
    den_grad = -lax.optimization_barrier(jnp.sum(grad_float * hidden, axis=2)) * denominator / (norm_value * norm_value)
    pair_grad = contract('htv,hsv->hts', num_grad, values) + den_grad[:, :, None]
    score_grad = (weight * pair_grad).astype(jnp.bfloat16)
    query_grad = contract('hts,hsd->htd', score_grad, keys) * query_scale
    key_grad = contract('hts,htd->hsd', score_grad, query) * query_scale
    value_grad = contract('hts,htv->hsv', pair_weight, num_grad)
    query_beta = (beta_weight[:, :, None] * query.astype(jnp.float32) * query_scale).astype(jnp.bfloat16)
    adjoint = contract('htd,htv->hdv', query_beta, num_grad)
    adjoint_n = lax.optimization_barrier(jnp.sum(query_beta.astype(jnp.float32) * den_grad[:, :, None], axis=1))
    return (num_grad, den_grad, query_grad, key_grad, value_grad, adjoint, adjoint_n)

def block_grads(query, keys, values, num_grad, den_grad, beta_weight, alpha_weight, state_bf, state_n_bf, query_grad, key_grad, value_grad, back_in, back_n_in):
    query_scale = query.shape[2] ** (-0.5)
    back_bf = back_in.astype(jnp.bfloat16)
    back_n_bf = back_n_in.astype(jnp.bfloat16)
    from_state = contract('htv,hdv->htd', num_grad, state_bf) + den_grad[:, :, None] * state_n_bf.astype(jnp.float32)[:, None, :]
    query_grad = query_grad + beta_weight[:, :, None] * from_state * query_scale
    from_back = contract('hsv,hdv->hsd', values, back_bf) + back_n_bf.astype(jnp.float32)[:, None, :]
    key_grad = key_grad + alpha_weight[:, :, None] * from_back
    value_grad = value_grad + alpha_weight[:, :, None] * contract('hsd,hdv->hsv', keys, back_bf)
    row_term = lax.optimization_barrier(jnp.sum(query.astype(jnp.float32) * query_grad, axis=2))
    key_term = lax.optimization_barrier(jnp.sum(keys.astype(jnp.float32) * key_grad, axis=2))
    return (query_grad, key_grad, value_grad, row_term, key_term)

def to_blocks(array):
    shaped = array.reshape((array.shape[0], N_CTX, array.shape[1] // N_CTX) + array.shape[2:])
    return jnp.moveaxis(shaped, 1, 0)

def from_blocks(array):
    moved = jnp.moveaxis(array, 0, 1)
    return moved.reshape((moved.shape[0], moved.shape[1] * moved.shape[2]) + moved.shape[3:])

def carry_step(carried, block_item):
    state_in, state_n_in = carried
    update, update_n, decay_factor = block_item
    following = (decay_factor[:, None, None] * state_in + update, decay_factor[:, None] * state_n_in + update_n)
    return (following, (state_in, state_n_in))

def reference(query, keys, values, igate, fgate, hidden_output_gradient, doc_start):
    inputs = tuple((to_blocks(member) for member in (query, keys, values, igate, fgate, hidden_output_gradient)))
    inputs = inputs + (doc_start.reshape(N_CTX, -1),)

    def first_pass(block_item):
        query_block, keys_block, values_block, igate_block, fgate_block, grad_block, starts_block = block_item
        local_parts = block_local(query_block, keys_block, values_block, igate_block, fgate_block, starts_block)
        return (local_parts[5], local_parts[6], local_parts[4])
    update_all, update_n_all, decay_all = lax.map(first_pass, inputs)
    zero_state = (jnp.zeros((HEAD_COUNT, DQK, DV), jnp.float32), jnp.zeros((HEAD_COUNT, DQK), jnp.float32))
    unused_state, (state_all, state_n_all) = lax.scan(carry_step, zero_state, (update_all, update_n_all, decay_all))

    def second_pass(block_item):
        query_block, keys_block, values_block, igate_block, fgate_block, grad_block, starts_block, state_in, state_n_in = block_item
        weight, pair_weight, alpha_weight, beta_weight, decay_factor, update, update_n = block_local(query_block, keys_block, values_block, igate_block, fgate_block, starts_block)
        hidden, denominator, norm_value, state_bf, state_n_bf = block_output(query_block, values_block, pair_weight, beta_weight, state_in, state_n_in)
        parts = block_backward(query_block, keys_block, values_block, grad_block, weight, pair_weight, beta_weight, hidden, denominator, norm_value)
        return (parts[5], parts[6])
    adjoint_all, adjoint_n_all = lax.map(second_pass, inputs + (state_all, state_n_all))
    unused_back, (back_all, back_n_all) = lax.scan(carry_step, zero_state, (adjoint_all, adjoint_n_all, decay_all), reverse=True)

    def third_pass(block_item):
        query_block, keys_block, values_block, igate_block, fgate_block, grad_block, starts_block, state_in, state_n_in, back_in, back_n_in = block_item
        weight, pair_weight, alpha_weight, beta_weight, decay_factor, update, update_n = block_local(query_block, keys_block, values_block, igate_block, fgate_block, starts_block)
        hidden, denominator, norm_value, state_bf, state_n_bf = block_output(query_block, values_block, pair_weight, beta_weight, state_in, state_n_in)
        num_grad, den_grad, query_grad, key_grad, value_grad, adjoint, adjoint_n = block_backward(query_block, keys_block, values_block, grad_block, weight, pair_weight, beta_weight, hidden, denominator, norm_value)
        query_grad, key_grad, value_grad, row_term, key_term = block_grads(query_block, keys_block, values_block, num_grad, den_grad, beta_weight, alpha_weight, state_bf, state_n_bf, query_grad, key_grad, value_grad, back_in, back_n_in)
        return (hidden.astype(jnp.bfloat16), query_grad.astype(jnp.bfloat16), key_grad.astype(jnp.bfloat16), value_grad.astype(jnp.bfloat16), key_term, row_term - key_term)
    results = lax.map(third_pass, inputs + (state_all, state_n_all, back_all, back_n_all))
    hidden_out, grad_query, grad_keys, grad_values, key_term, gate_term = (from_blocks(member) for member in results)
    forget_grad = jnp.flip(jnp.cumsum(jnp.flip(gate_term, 1), axis=1), 1)
    grad_fgate = (forget_grad * jax.nn.sigmoid(-fgate.astype(jnp.float32))).astype(jnp.bfloat16)
    input_gate_gradient = key_term.astype(jnp.bfloat16)
    return (hidden_out, grad_query, grad_keys, grad_values, input_gate_gradient, grad_fgate)
```

```python
import functools

import jax
import jax.numpy as jnp
from jax import lax
from jax.experimental import pallas as pl
from jax.experimental.pallas import tpu as pltpu
from jax.sharding import PartitionSpec as P

f32, bf16 = jnp.float32, jnp.bfloat16
CHUNK, CHUNKS, TOKENS = 128, 4, 512
HEADS = 2
DK, DV = 256, 512
WIDE = DK + DV
EXTRA = 16
SLICES = 32
NEG = -1e30
SCALE = DK ** (-0.5)
ROWS = 256
VMEM = pltpu.VMEM
PARAMS = pltpu.CompilerParams(vmem_limit_bytes=56 * 1024 * 1024)


def dot(left, right, cl, cr, precision=None):
    return lax.dot_general(
        left, right, (((cl,), (cr,)), ((), ())), preferred_element_type=f32, precision=precision
    )


def exact(left, right):
    return dot(left, right, 1, 0, lax.Precision.HIGHEST)


def column(bundle, first):
    return jnp.concatenate([bundle[:, first + c : first + c + 1] for c in range(CHUNKS)], axis=0)


def line(bundle, first):
    return jnp.concatenate([bundle[first + c : first + c + 1, :] for c in range(CHUNKS)], axis=1)


def chunk_of(y, shift):
    return lax.rem(y + shift + CHUNKS, CHUNKS)


def smem():
    return pl.BlockSpec(memory_space=pltpu.SMEM)


def whole():
    return pl.BlockSpec(memory_space=VMEM)


def call(body, outs, ins, scratch=(), flops=0, grid_spec=None):
    size = lambda s: functools.reduce(lambda a, b: a * b, s.shape, 1) * s.dtype.itemsize
    args = dict(
        out_shape=outs,
        compiler_params=PARAMS,
        cost_estimate=pl.CostEstimate(
            flops=flops,
            bytes_accessed=sum(size(s) for s in list(ins) + list(outs)),
            transcendentals=0,
        ),
    )
    if grid_spec is not None:
        return pl.pallas_call(body, grid_spec=grid_spec, **args)(*ins)
    return pl.pallas_call(
        body,
        in_specs=[smem() if a.dtype == jnp.int32 and a.size <= 2 else whole() for a in ins],
        out_specs=tuple(whole() for _ in outs),
        scratch_shapes=scratch,
        **args,
    )(*ins)


def like(shape, dtype):
    return jax.ShapeDtypeStruct(shape, dtype)


def pack_body(gates, y_ref, a_ref, b_ref, *rest):
    outs = rest[-3:]
    y = y_ref[0]
    for shift, out in enumerate(outs, 1):
        dest = chunk_of(y, shift)
        for h in range(HEADS):
            out[h * CHUNK : (h + 1) * CHUNK, 0:DK] = a_ref[dest * HEADS + h]
            out[h * CHUNK : (h + 1) * CHUNK, DK:WIDE] = b_ref[dest * HEADS + h]
        if gates:
            both = jnp.concatenate([rest[0][...].astype(f32), rest[1][...].astype(f32)], axis=0)
            out[HEADS * CHUNK : HEADS * CHUNK + EXTRA, 0:CHUNK] = both.astype(bf16)


def pack(y, narrow, wide, gates=()):
    rows = HEADS * CHUNK + (EXTRA if gates else 0)
    return call(
        functools.partial(pack_body, bool(gates)),
        [like((rows, WIDE), bf16)] * 3,
        [y, narrow, wide, *gates],
    )


def assemble(all_ref, y, narrow_ref, wide_ref, received):
    for h in range(HEADS):
        all_ref[h, y, :, 0:DK] = narrow_ref[h]
        all_ref[h, y, :, DK:WIDE] = wide_ref[h]
    for shift, ref in enumerate(received, 1):
        source = chunk_of(y, -shift)
        for h in range(HEADS):
            all_ref[h, source] = ref[h * CHUNK : (h + 1) * CHUNK, :]


def update_body(
    y_ref, k_ref, v_ref, kv1, kv2, kv3, ig_ref, fg_ref, doc_ref, all_ref, line_ref, col_ref, pay_ref, gates, lines, extra
):
    y = y_ref[0]
    assemble(all_ref, y, k_ref, v_ref, (kv1, kv2, kv3))
    gates[y] = jnp.concatenate([ig_ref[...].astype(f32), fg_ref[...].astype(f32)], axis=0)
    for shift, ref in enumerate((kv1, kv2, kv3), 1):
        gates[chunk_of(y, -shift)] = ref[HEADS * CHUNK : HEADS * CHUNK + EXTRA, 0:CHUNK].astype(f32)
    row = lax.broadcasted_iota(jnp.int32, (16, CHUNK), 0)
    for c in range(CHUNKS):
        tile = gates[c]
        for h in range(HEADS):
            pick = y * HEADS + h
            lines[1, h * CHUNKS + c : h * CHUNKS + c + 1, :] = jnp.sum(
                jnp.where(row == pick, tile, 0.0), axis=0, keepdims=True
            )
            lines[0, h * CHUNKS + c : h * CHUNKS + c + 1, :] = jnp.sum(
                jnp.where(row == pick + 8, tile, 0.0), axis=0, keepdims=True
            )
    forget = lines[0, 0:8]
    fade = jnp.exp(-forget)
    lines[0, 0:8] = -jnp.log1p(fade)
    lines[0, 8:12] = doc_ref[...].astype(f32)
    lines[0, 12:16] = jnp.zeros((4, CHUNK), f32)
    closed = fade / (1.0 + fade)
    before = lax.broadcasted_iota(jnp.int32, (CHUNK, CHUNK), 0)
    after = lax.broadcasted_iota(jnp.int32, (CHUNK, CHUNK), 1)
    total = exact(lines[0], (before <= after).astype(f32))
    whole_lines = []
    for group in range(3):
        run = jnp.zeros((1, 1), f32)
        for c in range(CHUNKS):
            here = total[group * CHUNKS + c : group * CHUNKS + c + 1, :]
            whole_lines.append(here + run)
            run = run + here[:, CHUNK - 1 : CHUNK]
    segment = jnp.concatenate(whole_lines[8:12], axis=0)
    segment_end = segment[3:4, CHUNK - 1 : CHUNK]
    extra[...] = jnp.zeros_like(extra)
    for h in range(HEADS):
        cumulative = jnp.concatenate(whole_lines[h * CHUNKS : (h + 1) * CHUNKS], axis=0)
        end = cumulative[3:4, CHUNK - 1 : CHUNK]
        ingate = lines[1, h * CHUNKS : (h + 1) * CHUNKS]
        line_ref[h] = jnp.zeros((CHUNK, CHUNK), f32)
        line_ref[h, 0:4] = cumulative
        line_ref[h, 4:8] = ingate - cumulative
        line_ref[h, 8:12] = jnp.where(segment == segment_end, jnp.exp(end - cumulative + ingate), 0.0)
        line_ref[h, 12:16] = jnp.where(segment == 0.0, jnp.exp(cumulative), 0.0)
        line_ref[h, 16:20] = segment
        line_ref[h, 20:24] = closed[h * CHUNKS : (h + 1) * CHUNKS]
        col_ref[h] = line_ref[h].T
        decay = jnp.where(segment_end == 0.0, jnp.exp(end), 0.0)
        keys = all_ref[h, :, :, 0:DK].reshape(TOKENS, DK)
        values = all_ref[h, :, :, DK:WIDE].reshape(TOKENS, DV)
        keys_alpha = (column(col_ref[h], 8) * keys.astype(f32)).astype(bf16)
        update = dot(keys_alpha, values, 0, 0).astype(bf16)
        scatter(pay_ref, update, h)
        update_n = jnp.sum(keys_alpha.astype(f32), axis=0, keepdims=True)
        for half in range(2):
            extra[2 * h + half : 2 * h + half + 1, :] = update_n[:, half * CHUNK : (half + 1) * CHUNK]
            extra[4 + 2 * h + half : 5 + 2 * h + half, :] = jnp.broadcast_to(decay, (1, CHUNK))
    high = extra[...].astype(bf16)
    low = extra[...] - high.astype(f32)
    tile = jnp.concatenate([high.astype(f32), low], axis=0).astype(bf16)
    for i in range(SLICES):
        pay_ref[i, :, 2 * DK : 2 * DK + CHUNK] = tile


def scatter(pay_ref, matrix, h):
    for i in range(SLICES):
        r, c = i // 2, i % 2
        pay_ref[i, :, h * DK : (h + 1) * DK] = matrix[16 * r : 16 * (r + 1), DK * c : DK * (c + 1)]


def collect(matrix_ref, pay_ref, h):
    for i in range(SLICES):
        r, c = i // 2, i % 2
        matrix_ref[h, 16 * r : 16 * (r + 1), DK * c : DK * (c + 1)] = pay_ref[i, :, h * DK : (h + 1) * DK]


def spread(extra):
    return jnp.concatenate([extra[4 + r : 5 + r, :] for r in range(4)], axis=1)


def state_scan_body(n_ctx, me_ref, in_ref, out_ref, norm_ref, extra_ref):
    mine = SLICES // n_ctx
    me = me_ref[0]
    state = jnp.zeros((mine, 16, 2 * DK), f32)
    norm = jnp.zeros((4, CHUNK), f32)
    for j in range(n_ctx):
        block = in_ref[j * mine : (j + 1) * mine, :, 0 : 2 * DK]
        tile = in_ref[j * mine, :, 2 * DK : 2 * DK + CHUNK].astype(f32)
        extra = tile[0:8] + tile[8:16]
        extra_ref[j] = extra
        out_ref[j * mine : (j + 1) * mine] = state.astype(bf16)
        state = spread(extra) * state + block.astype(f32)
        norm = jnp.where(j < me, extra[4:8] * norm + extra[0:4], norm)
    norm_ref[...] = jnp.concatenate([norm, jnp.zeros((4, CHUNK), f32)], axis=0)


def back_scan_body(n_ctx, in_ref, extra_ref, out_ref):
    mine = SLICES // n_ctx
    back = jnp.zeros((mine, 16, 2 * DK), f32)
    for j in reversed(range(n_ctx)):
        block = in_ref[j * mine : (j + 1) * mine]
        out_ref[j * mine : (j + 1) * mine] = back.astype(bf16)
        back = spread(extra_ref[j]) * back + block.astype(f32)


def weights(line_ref, col_ref, h, r):
    last = (r + 1) * ROWS
    here = slice(r * ROWS, last)
    position = lax.broadcasted_iota(jnp.int32, (ROWS, last), 0) + r * ROWS
    source = lax.broadcasted_iota(jnp.int32, (ROWS, last), 1)
    log_weight = column(col_ref[h], 0)[here] + line(line_ref[h], 4)[:, 0:last]
    allowed = (position >= source) & (column(col_ref[h], 16)[here] == line(line_ref[h], 16)[:, 0:last])
    return jnp.exp(jnp.where(allowed, log_weight, NEG))


def put_column(ref, h, first, value):
    for c in range(CHUNKS):
        ref[h, :, first + c : first + c + 1] = value[c * CHUNK : (c + 1) * CHUNK]


def norm_line(norm_ref, h):
    both = [norm_ref[2 * h + half : 2 * h + half + 1, :] for half in range(2)]
    return jnp.concatenate(both, axis=1).astype(bf16).astype(f32)


def adjoint_body(
    y_ref, q_ref, g_ref, qg1, qg2, qg3, kv_ref, line_ref, col_ref, norm_ref, all_ref, pair_ref, num_ref, cols_ref, pay_ref
):
    assemble(all_ref, y_ref[0], q_ref, g_ref, (qg1, qg2, qg3))
    for h in range(HEADS):
        cols_ref[h] = jnp.zeros((CHUNK, CHUNK), f32)
        keys = kv_ref[h, :, :, 0:DK].reshape(TOKENS, DK)
        query = all_ref[h, :, :, 0:DK].reshape(TOKENS, DK)
        sums = []
        for r in range(TOKENS // ROWS):
            last = (r + 1) * ROWS
            scores = dot(query[r * ROWS : last], keys[0:last], 1, 1) * SCALE
            pair = (weights(line_ref, col_ref, h, r) * scores).astype(bf16)
            pair_ref[h, r * ROWS : last, 0:last] = pair
            if last < TOKENS:
                pair_ref[h, r * ROWS : last, last:TOKENS] = jnp.zeros((ROWS, TOKENS - last), bf16)
            sums.append(jnp.sum(pair.astype(f32), axis=1, keepdims=True))
        beta = column(col_ref[h], 12)
        wide_query = query.astype(f32)
        cross = jnp.sum(wide_query * norm_line(norm_ref, h), axis=1, keepdims=True)
        denominator = jnp.concatenate(sums, axis=0) + beta * cross * SCALE
        norm = jnp.sqrt(denominator * denominator + 1.0)
        put_column(cols_ref, h, 0, denominator)
        put_column(cols_ref, h, 4, norm)
        grad = all_ref[h, :, :, DK:WIDE].reshape(TOKENS, DV).astype(f32)
        num_grad = (grad / norm).astype(bf16)
        num_ref[h] = num_grad
        query_beta = (beta * wide_query * SCALE).astype(bf16)
        scatter(pay_ref, dot(query_beta, num_grad, 0, 0).astype(bf16), h)


def hidden_body(
    y_ref, kv_ref, qg_ref, pair_ref, num_ref, line_ref, col_ref, norm_ref, cols_ref, in_ref, o0, o1, o2, o3, score_ref, terms_ref, adjoint_ref, state, done
):
    y = y_ref[0]
    adjoint = []
    for h in range(HEADS):
        collect(state, in_ref, h)
        state_bf = state[h]
        terms_ref[h] = jnp.zeros((CHUNK, CHUNK), f32)
        keys = kv_ref[h, :, :, 0:DK].reshape(TOKENS, DK)
        values = kv_ref[h, :, :, DK:WIDE].reshape(TOKENS, DV)
        query = qg_ref[h, :, :, 0:DK].reshape(TOKENS, DK)
        grad = qg_ref[h, :, :, DK:WIDE].reshape(TOKENS, DV)
        beta = column(col_ref[h], 12)
        denominator = column(cols_ref[h], 0)
        norm = column(cols_ref[h], 4)
        norm_bf = norm_line(norm_ref, h)
        total = jnp.zeros((1, DK), f32)
        rows = []
        for r in range(TOKENS // ROWS):
            last = (r + 1) * ROWS
            here = slice(r * ROWS, last)
            cross = dot(query[here], state_bf, 1, 0)
            numerator = dot(pair_ref[h, here, 0:last], values[0:last], 1, 0) + beta[here] * cross * SCALE
            hidden = numerator / norm[here]
            done[here, 0:DV] = hidden.astype(bf16)
            inner = jnp.sum(grad[here].astype(f32) * hidden, axis=1, keepdims=True)
            den_grad = -inner * denominator[here] / (norm[here] * norm[here])
            wide_query = query[here].astype(f32)
            query_beta = (beta[here] * wide_query * SCALE).astype(bf16).astype(f32)
            total = total + jnp.sum(query_beta * den_grad, axis=0, keepdims=True)
            num_grad = num_ref[h, here]
            pair_grad = dot(num_grad, values[0:last], 1, 1) + den_grad
            score = (weights(line_ref, col_ref, h, r) * pair_grad).astype(bf16)
            score_ref[h, here, 0:last] = score
            if last < TOKENS:
                score_ref[h, here, last:TOKENS] = jnp.zeros((ROWS, TOKENS - last), bf16)
            from_state = dot(num_grad, state_bf, 1, 1) + den_grad * norm_bf
            query_grad = dot(score, keys[0:last], 1, 0) * SCALE + beta[here] * from_state * SCALE
            done[here, DV : DV + DK] = query_grad.astype(bf16)
            rows.append(jnp.sum(wide_query * query_grad, axis=1, keepdims=True))
        put_column(terms_ref, h, 0, jnp.concatenate(rows, axis=0))
        adjoint += [total[:, 0:CHUNK], total[:, CHUNK:DK]]
        send(done, y, h, (o0, o1, o2, o3))
    adjoint = jnp.concatenate(adjoint + [jnp.zeros((4, CHUNK), f32)], axis=0)
    for i in range(adjoint_ref.shape[0]):
        adjoint_ref[i] = adjoint


def send(done, y, h, outs):
    for shift, out in enumerate(outs):
        first = pl.multiple_of(chunk_of(y, shift) * CHUNK, CHUNK)
        out[h * CHUNK : (h + 1) * CHUNK, :] = done[pl.ds(first, CHUNK), :]


def local_body(qg_ref, pair_ref, num_ref, score_ref, key_ref, value_ref):
    for h in range(HEADS):
        query = qg_ref[h, :, :, 0:DK].reshape(TOKENS, DK)
        for s in range(TOKENS // ROWS):
            here = slice(s * ROWS, (s + 1) * ROWS)
            first = s * ROWS
            key_ref[h, here] = dot(score_ref[h, first:TOKENS, here], query[first:TOKENS], 0, 0) * SCALE
            value_ref[h, here] = dot(pair_ref[h, first:TOKENS, here], num_ref[h, first:TOKENS], 0, 0)


def grads_body(
    n_ctx, y_ref, me_ref, kv_ref, key_ref, value_ref, line_ref, col_ref, terms_ref, state_ref, pay_ref, back_ref, norm_ref, extra_ref, adjoint_ref, o0, o1, o2, o3, back, done, cols
):
    y, me = y_ref[0], me_ref[0]
    norm = jnp.zeros((4, CHUNK), f32)
    for j in reversed(range(n_ctx)):
        norm = jnp.where(j > me, extra_ref[j][4:8] * norm + adjoint_ref[j][0:4], norm)
    back_n = norm.astype(bf16).astype(f32)
    extra = extra_ref[me]
    state_n = norm_ref[0:4, :].astype(bf16).astype(f32)
    later_n = (extra[4:8] * state_n + extra[0:4]) * back_n
    decay = spread(extra)
    later = jnp.zeros((16, 2 * DK), f32)
    for i in range(SLICES):
        state = decay * state_ref[i].astype(f32) + pay_ref[i, :, 0 : 2 * DK].astype(f32)
        later = later + state * back_ref[i].astype(f32)
    cols[...] = jnp.zeros_like(cols)
    for h in range(HEADS):
        collect(back, back_ref, h)
        back_bf = back[h]
        keys = kv_ref[h, :, :, 0:DK].reshape(TOKENS, DK)
        values = kv_ref[h, :, :, DK:WIDE].reshape(TOKENS, DV)
        alpha = column(col_ref[h], 8)
        row = jnp.concatenate([back_n[2 * h : 2 * h + 1], back_n[2 * h + 1 : 2 * h + 2]], axis=1)
        key_grad = key_ref[h] + alpha * (dot(values, back_bf, 1, 1) + row)
        value_grad = value_ref[h] + alpha * dot(keys, back_bf, 1, 0)
        done[:, 0:DV] = value_grad.astype(bf16)
        done[:, DV : DV + DK] = key_grad.astype(bf16)
        send(done, y, h, (o0, o1, o2, o3))
        key_term = jnp.sum(keys.astype(f32) * key_grad, axis=1, keepdims=True)
        for c in range(CHUNKS):
            piece = key_term[c * CHUNK : (c + 1) * CHUNK]
            cols[:, h * 4 + c : h * 4 + c + 1] = terms_ref[h, :, c : c + 1] - piece
            cols[:, 8 + h * 4 + c : 9 + h * 4 + c] = piece
    lines = cols[...].T[0:16]
    before = lax.broadcasted_iota(jnp.int32, (CHUNK, CHUNK), 0)
    after = lax.broadcasted_iota(jnp.int32, (CHUNK, CHUNK), 1)
    suffix = exact(lines, (before >= after).astype(f32))
    tiles = [[None] * HEADS for _ in range(CHUNKS)]
    for h in range(HEADS):
        run = jnp.sum(later[:, h * DK : (h + 1) * DK], keepdims=True) + jnp.sum(
            later_n[2 * h : 2 * h + 2], keepdims=True
        )
        for c in reversed(range(CHUNKS)):
            here = suffix[h * 4 + c : h * 4 + c + 1]
            tiles[c][h] = (here + run) * line_ref[h, 20 + c : 21 + c]
            run = run + here[:, 0:1]
    gates = jnp.zeros((CHUNKS, 16, CHUNK), f32)
    for c in range(CHUNKS):
        rows = [lines[8 + h * 4 + c : 9 + h * 4 + c] for h in range(HEADS)] + tiles[c]
        cols[c * 16 : (c + 1) * 16, :] = jnp.concatenate(rows + [jnp.zeros((12, CHUNK), f32)], axis=0)
    for shift, out in enumerate((o0, o1, o2, o3)):
        first = pl.multiple_of(chunk_of(y, shift) * 16, 16)
        out[HEADS * CHUNK : HEADS * CHUNK + EXTRA, 0:CHUNK] = cols[pl.ds(first, 16), :].astype(bf16)


def unpack_body(gates, y_ref, r0, r1, r2, r3, wide_ref, narrow_ref, *gate_refs):
    y = y_ref[0]
    row = lax.broadcasted_iota(jnp.int32, (8, CHUNK), 0)
    sums = [jnp.zeros((8, CHUNK), f32)] * 2
    for shift, ref in enumerate((r0, r1, r2, r3)):
        source = chunk_of(y, -shift)
        for h in range(HEADS):
            wide_ref[source * HEADS + h] = ref[h * CHUNK : (h + 1) * CHUNK, 0:DV]
            narrow_ref[source * HEADS + h] = ref[h * CHUNK : (h + 1) * CHUNK, DV : DV + DK]
        if gates:
            tile = ref[HEADS * CHUNK : HEADS * CHUNK + EXTRA, 0:CHUNK].astype(f32)
            for k in range(2):
                for h in range(HEADS):
                    here = jnp.where(row == source * HEADS + h, tile[2 * k + h : 2 * k + h + 1], 0.0)
                    sums[k] = sums[k] + here
    if gates:
        gate_refs[0][...] = sums[0].astype(bf16)
        gate_refs[1][...] = sums[1].astype(bf16)


def unpack(y, parts, gates):
    outs = [like((CHUNKS * HEADS, CHUNK, DV), bf16), like((CHUNKS * HEADS, CHUNK, DK), bf16)]
    if gates:
        outs += [like((CHUNKS * HEADS, CHUNK), bf16)] * 2
    return call(functools.partial(unpack_body, gates), outs, [y, *parts])


def shift_all(parts):
    moved = []
    for shift, part in enumerate(parts, 1):
        pairs = [(i, (i + shift) % CHUNKS) for i in range(CHUNKS)]
        moved.append(lax.ppermute(part, "head", pairs))
    return moved


def own(narrow, wide, y):
    return [lax.dynamic_slice_in_dim(part, y * HEADS, HEADS, 0) for part in (narrow, wide)]


def exchange(part):
    return lax.all_to_all(part, "ctx", split_axis=0, concat_axis=0, tiled=True)


def shards(query, keys, values, igate, fgate, hidden_output_gradient, doc_start):
    n_ctx = lax.axis_size("ctx")
    pair_flops = TOKENS * TOKENS * HEADS * 2
    y_index = lax.axis_index("head").astype(jnp.int32)
    y = y_index.reshape(1)
    me = lax.axis_index("ctx").astype(jnp.int32).reshape(1)
    kv_sent = pack(y, keys, values, (igate, fgate))
    qg_sent = pack(y, query, hidden_output_gradient)
    kv_received = shift_all(kv_sent)
    qg_received = shift_all(qg_sent)
    tokens = (HEADS, CHUNKS, CHUNK, WIDE)
    bundle = like((HEADS, CHUNK, CHUNK), f32)
    kv, lines, cols, payload = call(
        update_body,
        [like(tokens, bf16), bundle, bundle, like((SLICES, 16, 2 * DK + CHUNK), bf16)],
        [y, *own(keys, values, y_index), *kv_received, igate, fgate, doc_start.reshape(CHUNKS, CHUNK)],
        [VMEM((CHUNKS, 16, CHUNK), f32), VMEM((2, 16, CHUNK), f32), VMEM((8, CHUNK), f32)],
        flops=TOKENS * DK * DV * HEADS * 2,
    )
    part = like((SLICES, 16, 2 * DK), bf16)
    state_part, norm, extra = call(
        functools.partial(state_scan_body, n_ctx),
        [part, like((8, CHUNK), f32), like((n_ctx, 8, CHUNK), f32)],
        [me, exchange(payload)],
    )
    state = exchange(state_part)
    square = like((HEADS, TOKENS, TOKENS), bf16)
    qg, pair, num_grad, norm_cols, adjoint = call(
        adjoint_body,
        [like(tokens, bf16), square, like((HEADS, TOKENS, DV), bf16), bundle, part],
        [y, *own(query, hidden_output_gradient, y_index), *qg_received, kv, lines, cols, norm],
        flops=pair_flops * DK + TOKENS * DK * DV * HEADS * 2,
    )
    (back_part,) = call(
        functools.partial(back_scan_body, n_ctx), [part], [exchange(adjoint), extra]
    )
    back = exchange(back_part)
    plain = like((HEADS * CHUNK, WIDE), bf16)
    *hidden_sent, score_grad, terms, adjoint_n = call(
        hidden_body,
        [plain] * 4 + [square, bundle, like((n_ctx, 8, CHUNK), f32)],
        [y, kv, qg, pair, num_grad, lines, cols, norm, norm_cols, state],
        [VMEM((HEADS, DK, DV), bf16), VMEM((TOKENS, WIDE), bf16)],
        flops=pair_flops * (DV + DV + DK) + 2 * TOKENS * DK * DV * HEADS * 2,
    )
    hidden_received = shift_all(hidden_sent[1:])
    adjoint_all = exchange(adjoint_n)
    key_grad, value_grad = call(
        local_body,
        [like((HEADS, TOKENS, DK), f32), like((HEADS, TOKENS, DV), f32)],
        [qg, pair, num_grad, score_grad],
        flops=pair_flops * (DK + DV),
    )
    grads_sent = call(
        functools.partial(grads_body, n_ctx),
        [like((HEADS * CHUNK + EXTRA, WIDE), bf16)] * 4,
        [y, me, kv, key_grad, value_grad, lines, cols, terms, state, payload, back, norm, extra, adjoint_all],
        [VMEM((HEADS, DK, DV), bf16), VMEM((TOKENS, WIDE), bf16), VMEM((CHUNK, CHUNK), f32)],
        flops=2 * TOKENS * DK * DV * HEADS * 2,
    )
    grads_received = shift_all(grads_sent[1:])
    hidden_home, query_home = unpack(y, [hidden_sent[0], *hidden_received], False)
    value_home, key_home, input_home, forget_home = unpack(y, [grads_sent[0], *grads_received], True)
    return (hidden_home, query_home, key_home, value_home, input_home, forget_home)


def solution(mesh):
    spec = P(None, ("ctx", "head"), None)
    flat = P(None, ("ctx", "head"))
    return jax.shard_map(
        shards,
        mesh=mesh,
        in_specs=(spec, spec, spec, flat, flat, spec, P("ctx")),
        out_specs=(spec, spec, spec, spec, flat, flat),
        check_vma=False,
    )
```

```python
import functools

import jax
import jax.numpy as jnp
from jax import lax
from jax.experimental import pallas as pl
from jax.experimental.pallas import tpu as pltpu
from jax.sharding import PartitionSpec as P

f32, bf16 = jnp.float32, jnp.bfloat16
CHUNK, CHUNKS, TOKENS = 128, 4, 512
HEADS = 2
DK, DV = 256, 512
WIDE = DK + DV
EXTRA = 16
SLICES = 32
NEG = -1e30
BIG = 10**8
SCALE = DK ** (-0.5)
ROWS = 256
VMEM = pltpu.VMEM
PARAMS = pltpu.CompilerParams(vmem_limit_bytes=16 * 1024 * 1024)


def dot(left, right, cl, cr, precision=None):
    return lax.dot_general(
        left, right, (((cl,), (cr,)), ((), ())), preferred_element_type=f32, precision=precision
    )


def exact(left, right):
    return dot(left, right, 1, 0, lax.Precision.HIGHEST)


def column(bundle, first):
    return jnp.concatenate([bundle[:, first + c : first + c + 1] for c in range(CHUNKS)], axis=0)


def line(bundle, first):
    return jnp.concatenate([bundle[first + c : first + c + 1, :] for c in range(CHUNKS)], axis=1)


def chunk_of(y, shift):
    return lax.rem(y + shift + CHUNKS, CHUNKS)


def smem():
    return pl.BlockSpec(memory_space=pltpu.SMEM)


def whole():
    return pl.BlockSpec(memory_space=VMEM)


def call(body, outs, ins, scratch=(), cost=1, after=()):
    def run(*refs):
        body(*refs[: len(ins)], *refs[len(ins) + len(after) :])

    in_specs = [smem() if a.dtype == jnp.int32 and a.size <= 2 else whole() for a in ins]
    return pl.pallas_call(
        run,
        out_shape=outs,
        in_specs=in_specs + [pl.BlockSpec(memory_space=pl.ANY) for _ in after],
        out_specs=tuple(whole() for _ in outs),
        scratch_shapes=scratch,
        compiler_params=PARAMS,
        cost_estimate=pl.CostEstimate(flops=cost, bytes_accessed=cost, transcendentals=0),
    )(*ins, *after)


def like(shape, dtype):
    return jax.ShapeDtypeStruct(shape, dtype)


def pack_body(gates, y_ref, a_ref, b_ref, *rest):
    outs = rest[-4:]
    y = y_ref[0]
    for shift, out in enumerate(outs):
        dest = chunk_of(y, shift)
        for h in range(HEADS):
            out[h * CHUNK : (h + 1) * CHUNK, 0:DK] = a_ref[dest * HEADS + h]
            out[h * CHUNK : (h + 1) * CHUNK, DK:WIDE] = b_ref[dest * HEADS + h]
        if gates:
            both = jnp.concatenate([rest[0][...].astype(f32), rest[1][...].astype(f32)], axis=0)
            out[HEADS * CHUNK : HEADS * CHUNK + EXTRA, 0:CHUNK] = both.astype(bf16)


def pack(y, narrow, wide, gates=()):
    rows = HEADS * CHUNK + (EXTRA if gates else 0)
    return call(
        functools.partial(pack_body, bool(gates)),
        [like((rows, WIDE), bf16)] * 4,
        [y, narrow, wide, *gates],
    )


def assemble(all_ref, y, received):
    for shift, ref in enumerate(received):
        source = chunk_of(y, -shift)
        for h in range(HEADS):
            all_ref[h, source] = ref[h * CHUNK : (h + 1) * CHUNK, :]


def update_body(
    y_ref, kv0, kv1, kv2, kv3, doc_ref, all_ref, line_ref, col_ref, pay_ref, gates, lines, extra
):
    y = y_ref[0]
    received = (kv0, kv1, kv2, kv3)
    assemble(all_ref, y, received)
    for shift, ref in enumerate(received):
        gates[chunk_of(y, -shift)] = ref[HEADS * CHUNK : HEADS * CHUNK + EXTRA, 0:CHUNK].astype(f32)
    row = lax.broadcasted_iota(jnp.int32, (16, CHUNK), 0)
    for c in range(CHUNKS):
        tile = gates[c]
        for h in range(HEADS):
            pick = y * HEADS + h
            lines[1, h * CHUNKS + c : h * CHUNKS + c + 1, :] = jnp.sum(
                jnp.where(row == pick, tile, 0.0), axis=0, keepdims=True
            )
            lines[0, h * CHUNKS + c : h * CHUNKS + c + 1, :] = jnp.sum(
                jnp.where(row == pick + 8, tile, 0.0), axis=0, keepdims=True
            )
    forget = lines[0, 0:8]
    fade = jnp.exp(-forget)
    lines[0, 0:8] = -jnp.log1p(fade)
    lines[0, 8:12] = doc_ref[...].astype(f32)
    lines[0, 12:16] = jnp.zeros((4, CHUNK), f32)
    closed = fade / (1.0 + fade)
    before = lax.broadcasted_iota(jnp.int32, (CHUNK, CHUNK), 0)
    after = lax.broadcasted_iota(jnp.int32, (CHUNK, CHUNK), 1)
    total = exact(lines[0], (before <= after).astype(f32))
    whole_lines = []
    for group in range(3):
        run = jnp.zeros((1, 1), f32)
        for c in range(CHUNKS):
            here = total[group * CHUNKS + c : group * CHUNKS + c + 1, :]
            whole_lines.append(here + run)
            run = run + here[:, CHUNK - 1 : CHUNK]
    segment = jnp.concatenate(whole_lines[8:12], axis=0)
    segment_end = segment[3:4, CHUNK - 1 : CHUNK]
    extra[...] = jnp.zeros_like(extra)
    for h in range(HEADS):
        cumulative = jnp.concatenate(whole_lines[h * CHUNKS : (h + 1) * CHUNKS], axis=0)
        end = cumulative[3:4, CHUNK - 1 : CHUNK]
        ingate = lines[1, h * CHUNKS : (h + 1) * CHUNKS]
        line_ref[h] = jnp.zeros((CHUNK, CHUNK), f32)
        line_ref[h, 0:4] = cumulative
        line_ref[h, 4:8] = ingate - cumulative
        line_ref[h, 8:12] = jnp.where(segment == segment_end, jnp.exp(end - cumulative + ingate), 0.0)
        line_ref[h, 12:16] = jnp.where(segment == 0.0, jnp.exp(cumulative), 0.0)
        line_ref[h, 16:20] = segment
        line_ref[h, 20:24] = closed[h * CHUNKS : (h + 1) * CHUNKS]
        col_ref[h] = line_ref[h].T
        decay = jnp.where(segment_end == 0.0, jnp.exp(end), 0.0)
        keys = all_ref[h, :, :, 0:DK].reshape(TOKENS, DK)
        values = all_ref[h, :, :, DK:WIDE].reshape(TOKENS, DV)
        keys_alpha = (column(col_ref[h], 8) * keys.astype(f32)).astype(bf16)
        update = dot(keys_alpha, values, 0, 0).astype(bf16)
        scatter(pay_ref, update, h)
        update_n = jnp.sum(keys_alpha.astype(f32), axis=0, keepdims=True)
        for half in range(2):
            extra[2 * h + half : 2 * h + half + 1, :] = update_n[:, half * CHUNK : (half + 1) * CHUNK]
            extra[4 + 2 * h + half : 5 + 2 * h + half, :] = jnp.broadcast_to(decay, (1, CHUNK))
    share(pay_ref, extra[...])


def share(pay_ref, lines):
    high = lines.astype(bf16).astype(f32)
    tile = jnp.concatenate([high, lines - high], axis=0).astype(bf16)
    for i in range(SLICES):
        pay_ref[i, :, 2 * DK : 2 * DK + CHUNK] = tile


def shared(pay_ref, index):
    tile = pay_ref[index, :, 2 * DK : 2 * DK + CHUNK].astype(f32)
    return tile[0:8] + tile[8:16]


def scatter(pay_ref, matrix, h, first=0):
    for i in range(SLICES):
        r, c = i // 2, i % 2
        here = slice(first + h * DK, first + (h + 1) * DK)
        pay_ref[i, :, here] = matrix[16 * r : 16 * (r + 1), DK * c : DK * (c + 1)]


def collect(matrix_ref, pay_ref, h):
    for i in range(SLICES):
        r, c = i // 2, i % 2
        matrix_ref[h, 16 * r : 16 * (r + 1), DK * c : DK * (c + 1)] = pay_ref[i, :, h * DK : (h + 1) * DK]


def pair_body(y_ref, qg0, qg1, qg2, qg3, kv_ref, line_ref, col_ref, all_ref, pair_ref, weight_ref, sum_ref):
    assemble(all_ref, y_ref[0], (qg0, qg1, qg2, qg3))
    for h in range(HEADS):
        sum_ref[h] = jnp.zeros((CHUNK, CHUNK), f32)
        keys = kv_ref[h, :, :, 0:DK].reshape(TOKENS, DK)
        query = all_ref[h, :, :, 0:DK].reshape(TOKENS, DK)
        for r in range(TOKENS // ROWS):
            last = (r + 1) * ROWS
            here = slice(r * ROWS, last)
            scores = dot(query[here], keys[0:last], 1, 1) * SCALE
            weight = weights(line_ref, col_ref, h, r)
            weight_ref[h, here, 0:last] = weight
            pair = (weight * scores).astype(bf16)
            pair_ref[h, here, 0:last] = pair
            put_column(sum_ref, h, 0, jnp.sum(pair.astype(f32), axis=1, keepdims=True), r)


def weights(line_ref, col_ref, h, r):
    last = (r + 1) * ROWS
    here = slice(r * ROWS, last)
    position = lax.broadcasted_iota(jnp.int32, (ROWS, last), 0) + r * ROWS
    source = lax.broadcasted_iota(jnp.int32, (ROWS, last), 1)
    log_weight = column(col_ref[h], 0)[here] + line(line_ref[h], 4)[:, 0:last]
    allowed = (position >= source) & (column(col_ref[h], 16)[here] == line(line_ref[h], 16)[:, 0:last])
    return jnp.exp(jnp.where(allowed, log_weight, NEG))


def put_column(ref, h, first, value, r=0):
    first += r * (ROWS // CHUNK)
    for c in range(value.shape[0] // CHUNK):
        ref[h, :, first + c : first + c + 1] = value[c * CHUNK : (c + 1) * CHUNK]


def norm_line(norm_ref, h):
    both = [norm_ref[2 * h + half : 2 * h + half + 1, :] for half in range(2)]
    return jnp.concatenate(both, axis=1).astype(bf16).astype(f32)


def spread(extra):
    return jnp.concatenate([extra[4 + r : 5 + r, :] for r in range(4)], axis=1)


def adjoint_body(n_ctx, me_ref, in_ref, qg_ref, col_ref, sum_ref, pay_ref, norm_ref, extra_ref, num_ref, cols_ref):
    mine = SLICES // n_ctx
    me = me_ref[0]
    norm = jnp.zeros((4, CHUNK), f32)
    for j in range(n_ctx):
        extra = shared(in_ref, j * mine)
        extra_ref[j] = extra
        norm = jnp.where(j < me, extra[4:8] * norm + extra[0:4], norm)
    norm_ref[...] = jnp.concatenate([norm, jnp.zeros((4, CHUNK), f32)], axis=0)
    for h in range(HEADS):
        cols_ref[h] = jnp.zeros((CHUNK, CHUNK), f32)
        query = qg_ref[h, :, :, 0:DK].reshape(TOKENS, DK).astype(f32)
        beta = column(col_ref[h], 12)
        cross = jnp.sum(query * norm_line(norm_ref, h), axis=1, keepdims=True)
        denominator = column(sum_ref[h], 0) + beta * cross * SCALE
        norm = jnp.sqrt(denominator * denominator + 1.0)
        put_column(cols_ref, h, 0, denominator)
        put_column(cols_ref, h, 4, norm)
        grad = qg_ref[h, :, :, DK:WIDE].reshape(TOKENS, DV).astype(f32)
        num_grad = (grad / norm).astype(bf16)
        num_ref[h] = num_grad
        query_beta = (beta * query * SCALE).astype(bf16)
        scatter(pay_ref, dot(query_beta, num_grad, 0, 0).astype(bf16), h, 2 * DK)
    state = jnp.zeros((mine, 16, 2 * DK), f32)
    for j in range(n_ctx):
        here = slice(j * mine, (j + 1) * mine)
        pay_ref[here, :, 0 : 2 * DK] = state.astype(bf16)
        state = spread(extra_ref[j]) * state + in_ref[here, :, 0 : 2 * DK].astype(f32)


def local_body(kv_ref, pair_ref, num_ref, weight_ref, inner_ref, score_ref, value_ref):
    for h in range(HEADS):
        values = kv_ref[h, :, :, DK:WIDE].reshape(TOKENS, DV)
        for r in range(TOKENS // ROWS):
            last = (r + 1) * ROWS
            here = slice(r * ROWS, last)
            inner_ref[h, here] = dot(pair_ref[h, here, 0:last], values[0:last], 1, 0)
            score_ref[h, here, 0:last] = weight_ref[h, here, 0:last] * dot(num_ref[h, here], values[0:last], 1, 1)
        for s in range(TOKENS // ROWS):
            first = s * ROWS
            here = slice(first, first + ROWS)
            value_ref[h, here] = dot(pair_ref[h, first:TOKENS, here], num_ref[h, first:TOKENS], 0, 0)


def hidden_body(
    n_ctx, y_ref, in_ref, extra_ref, qg_ref, inner_ref, col_ref, cols_ref, o0, o1, o2, o3, pay_ref, state_ref, den_ref, done, lines
):
    mine = SLICES // n_ctx
    lines[...] = jnp.zeros_like(lines)
    for h in range(HEADS):
        collect(state_ref, in_ref, h)
        state = state_ref[h]
        den_ref[h] = jnp.zeros((CHUNK, CHUNK), f32)
        beta = column(col_ref[h], 12) * SCALE
        denominator = column(cols_ref[h], 0)
        inverse = 1.0 / column(cols_ref[h], 4)
        factor = -denominator * inverse * inverse
        for r in range(TOKENS // ROWS):
            here = slice(r * ROWS, (r + 1) * ROWS)
            chunks = slice(r * ROWS // CHUNK, (r + 1) * ROWS // CHUNK)
            query = qg_ref[h, chunks, :, 0:DK].reshape(ROWS, DK)
            grad = qg_ref[h, chunks, :, DK:WIDE].reshape(ROWS, DV)
            hidden = (inner_ref[h, here] + beta[here] * dot(query, state, 1, 0)) * inverse[here]
            done[here, :] = hidden.astype(bf16)
            product = jnp.sum(grad.astype(f32) * hidden, axis=1, keepdims=True)
            den_grad = product * factor[here]
            put_column(den_ref, h, 0, den_grad, r)
            query_beta = (beta[here] * query.astype(f32)).astype(bf16).astype(f32)
            total = jnp.sum(query_beta * den_grad, axis=0, keepdims=True)
            for half in range(2):
                lines[2 * h + half : 2 * h + half + 1, :] += total[:, half * CHUNK : (half + 1) * CHUNK]
        send(done, y_ref[0], h, (o0, o1, o2, o3))
    share(pay_ref, lines[...])
    back = jnp.zeros((mine, 16, 2 * DK), f32)
    for j in reversed(range(n_ctx)):
        here = slice(j * mine, (j + 1) * mine)
        pay_ref[here, :, 0 : 2 * DK] = back.astype(bf16)
        back = spread(extra_ref[j]) * back + in_ref[here, :, 2 * DK : 4 * DK].astype(f32)


def send(done, y, h, outs):
    for shift, out in enumerate(outs):
        first = pl.multiple_of(chunk_of(y, shift) * CHUNK, CHUNK)
        out[h * CHUNK : (h + 1) * CHUNK, :] = done[pl.ds(first, CHUNK), :]


def score_body(
    y_ref, kv_ref, qg_ref, num_ref, weight_ref, inner_ref, state_ref, norm_ref, col_ref, den_ref, o0, o1, o2, o3, terms_ref, key_ref, score, done
):
    for h in range(HEADS):
        terms_ref[h] = jnp.zeros((CHUNK, CHUNK), f32)
        keys = kv_ref[h, :, :, 0:DK].reshape(TOKENS, DK)
        query = qg_ref[h, :, :, 0:DK].reshape(TOKENS, DK)
        beta = column(col_ref[h], 12) * SCALE
        den_grad = column(den_ref[h], 0)
        norm_bf = norm_line(norm_ref, h)
        state = state_ref[h]
        for r in range(TOKENS // ROWS):
            last = (r + 1) * ROWS
            here = slice(r * ROWS, last)
            score[here, 0:last] = (
                inner_ref[h, here, 0:last] + weight_ref[h, here, 0:last] * den_grad[here]
            ).astype(bf16)
            from_state = dot(num_ref[h, here], state, 1, 1) + den_grad[here] * norm_bf
            query_grad = dot(score[here, 0:last], keys[0:last], 1, 0) * SCALE + beta[here] * from_state
            done[here, :] = query_grad.astype(bf16)
            term = jnp.sum(query[here].astype(f32) * query_grad, axis=1, keepdims=True)
            put_column(terms_ref, h, 0, term, r)
        send(done, y_ref[0], h, (o0, o1, o2, o3))
        for s in range(TOKENS // ROWS):
            first = s * ROWS
            here = slice(first, first + ROWS)
            key_ref[h, here] = dot(score[first:TOKENS, here], query[first:TOKENS], 0, 0) * SCALE


def grads_body(
    n_ctx, y_ref, me_ref, in_ref, kv_ref, key_ref, value_ref, line_ref, col_ref, terms_ref, state_ref, pay_ref, norm_ref, extra_ref, o0, o1, o2, o3, back, done, cols
):
    mine = SLICES // n_ctx
    y, me = y_ref[0], me_ref[0]
    norm = jnp.zeros((4, CHUNK), f32)
    for j in reversed(range(n_ctx)):
        norm = jnp.where(j > me, extra_ref[j][4:8] * norm + shared(in_ref, j * mine)[0:4], norm)
    back_n = norm.astype(bf16).astype(f32)
    extra = extra_ref[me]
    state_n = norm_ref[0:4, :].astype(bf16).astype(f32)
    later_n = (extra[4:8] * state_n + extra[0:4]) * back_n
    decay = spread(extra)
    later = jnp.zeros((16, 2 * DK), f32)
    for i in range(SLICES):
        state = decay * state_ref[i, :, 0 : 2 * DK].astype(f32) + pay_ref[i, :, 0 : 2 * DK].astype(f32)
        later = later + state * in_ref[i, :, 0 : 2 * DK].astype(f32)
    cols[...] = jnp.zeros_like(cols)
    for h in range(HEADS):
        collect(back, in_ref, h)
        back_bf = back[h]
        keys = kv_ref[h, :, :, 0:DK].reshape(TOKENS, DK)
        values = kv_ref[h, :, :, DK:WIDE].reshape(TOKENS, DV)
        alpha = column(col_ref[h], 8)
        row = jnp.concatenate([back_n[2 * h : 2 * h + 1], back_n[2 * h + 1 : 2 * h + 2]], axis=1)
        for r in range(TOKENS // ROWS):
            here = slice(r * ROWS, (r + 1) * ROWS)
            key_grad = key_ref[h, here] + alpha[here] * (dot(values[here], back_bf, 1, 1) + row)
            value_grad = value_ref[h, here] + alpha[here] * dot(keys[here], back_bf, 1, 0)
            done[here, 0:DV] = value_grad.astype(bf16)
            done[here, DV : DV + DK] = key_grad.astype(bf16)
            key_term = jnp.sum(keys[here].astype(f32) * key_grad, axis=1, keepdims=True)
            for c in range(ROWS // CHUNK):
                piece = key_term[c * CHUNK : (c + 1) * CHUNK]
                k = r * (ROWS // CHUNK) + c
                cols[:, h * 4 + k : h * 4 + k + 1] = terms_ref[h, :, k : k + 1] - piece
                cols[:, 8 + h * 4 + k : 9 + h * 4 + k] = piece
        send(done, y, h, (o0, o1, o2, o3))
    lines = cols[...].T[0:16]
    before = lax.broadcasted_iota(jnp.int32, (CHUNK, CHUNK), 0)
    after = lax.broadcasted_iota(jnp.int32, (CHUNK, CHUNK), 1)
    suffix = exact(lines, (before >= after).astype(f32))
    tiles = [[None] * HEADS for _ in range(CHUNKS)]
    for h in range(HEADS):
        run = jnp.sum(later[:, h * DK : (h + 1) * DK], keepdims=True) + jnp.sum(
            later_n[2 * h : 2 * h + 2], keepdims=True
        )
        for c in reversed(range(CHUNKS)):
            here = suffix[h * 4 + c : h * 4 + c + 1]
            tiles[c][h] = (here + run) * line_ref[h, 20 + c : 21 + c]
            run = run + here[:, 0:1]
    for c in range(CHUNKS):
        rows = [lines[8 + h * 4 + c : 9 + h * 4 + c] for h in range(HEADS)] + tiles[c]
        cols[c * 16 : (c + 1) * 16, :] = jnp.concatenate(rows + [jnp.zeros((12, CHUNK), f32)], axis=0)
    for shift, out in enumerate((o0, o1, o2, o3)):
        first = pl.multiple_of(chunk_of(y, shift) * 16, 16)
        out[HEADS * CHUNK : HEADS * CHUNK + EXTRA, 0:CHUNK] = cols[pl.ds(first, 16), :].astype(bf16)


def unpack_plain_body(y_ref, r0, r1, r2, r3, out_ref):
    for shift, ref in enumerate((r0, r1, r2, r3)):
        source = chunk_of(y_ref[0], -shift)
        for h in range(HEADS):
            out_ref[source * HEADS + h] = ref[h * CHUNK : (h + 1) * CHUNK, :]


def unpack_body(y_ref, r0, r1, r2, r3, wide_ref, narrow_ref, input_ref, forget_ref):
    y = y_ref[0]
    row = lax.broadcasted_iota(jnp.int32, (8, CHUNK), 0)
    sums = [jnp.zeros((8, CHUNK), f32)] * 2
    for shift, ref in enumerate((r0, r1, r2, r3)):
        source = chunk_of(y, -shift)
        tile = ref[HEADS * CHUNK : HEADS * CHUNK + EXTRA, 0:CHUNK].astype(f32)
        for h in range(HEADS):
            wide_ref[source * HEADS + h] = ref[h * CHUNK : (h + 1) * CHUNK, 0:DV]
            narrow_ref[source * HEADS + h] = ref[h * CHUNK : (h + 1) * CHUNK, DV : DV + DK]
            for k in range(2):
                here = jnp.where(row == source * HEADS + h, tile[2 * k + h : 2 * k + h + 1], 0.0)
                sums[k] = sums[k] + here
    input_ref[...] = sums[0].astype(bf16)
    forget_ref[...] = sums[1].astype(bf16)


def shift_all(parts):
    moved = [parts[0]]
    for shift, part in enumerate(parts[1:], 1):
        pairs = [(i, (i + shift) % CHUNKS) for i in range(CHUNKS)]
        moved.append(lax.ppermute(part, "head", pairs))
    return moved


def exchange(part):
    return lax.all_to_all(part, "ctx", split_axis=0, concat_axis=0, tiled=True)


def shards(query, keys, values, igate, fgate, hidden_output_gradient, doc_start):
    n_ctx = lax.axis_size("ctx")
    y = lax.axis_index("head").astype(jnp.int32).reshape(1)
    me = lax.axis_index("ctx").astype(jnp.int32).reshape(1)
    kv_received = shift_all(pack(y, keys, values, (igate, fgate)))
    qg_received = shift_all(pack(y, query, hidden_output_gradient))
    tokens = like((HEADS, CHUNKS, CHUNK, WIDE), bf16)
    bundle = like((HEADS, CHUNK, CHUNK), f32)
    square = like((HEADS, TOKENS, TOKENS), f32)
    square_bf = like((HEADS, TOKENS, TOKENS), bf16)
    carried = like((SLICES, 16, 2 * DK + CHUNK), bf16)
    kv, lines, cols, payload = call(
        update_body,
        [tokens, bundle, bundle, carried],
        [y, *kv_received, doc_start.reshape(CHUNKS, CHUNK)],
        [VMEM((CHUNKS, 16, CHUNK), f32), VMEM((2, 16, CHUNK), f32), VMEM((8, CHUNK), f32)],
    )
    updates = exchange(payload)
    qg, pair, weight, sums = call(
        pair_body, [tokens, square_bf, square, bundle], [y, *qg_received, kv, lines, cols], cost=BIG
    )
    both, norm, extra, num_grad, norm_cols = call(
        functools.partial(adjoint_body, n_ctx),
        [
            like((SLICES, 16, 4 * DK), bf16),
            like((8, CHUNK), f32),
            like((n_ctx, 8, CHUNK), f32),
            like((HEADS, TOKENS, DV), bf16),
            bundle,
        ],
        [me, updates, qg, cols, sums],
    )
    states = exchange(both)
    wide = like((HEADS, TOKENS, DV), f32)
    inner, inner_score, value_grad = call(
        local_body, [wide, square, wide], [kv, pair, num_grad, weight], cost=BIG
    )
    hidden_part = like((HEADS * CHUNK, DV), bf16)
    *hidden_sent, back_part, state, den_grad = call(
        functools.partial(hidden_body, n_ctx),
        [hidden_part] * 4 + [carried, like((HEADS, DK, DV), bf16), bundle],
        [y, states, extra, qg, inner, cols, norm_cols],
        [VMEM((TOKENS, DV), bf16), VMEM((8, CHUNK), f32)],
    )
    backs = exchange(back_part)
    hidden_received = shift_all(hidden_sent)
    *query_sent, terms, key_grad = call(
        score_body,
        [like((HEADS * CHUNK, DK), bf16)] * 4 + [bundle, like((HEADS, TOKENS, DK), f32)],
        [y, kv, qg, num_grad, weight, inner_score, state, norm, cols, den_grad],
        [VMEM((TOKENS, TOKENS), bf16), VMEM((TOKENS, DK), bf16)],
        cost=BIG,
    )
    query_received = shift_all(query_sent)
    home = lambda width: like((CHUNKS * HEADS, CHUNK, width), bf16)
    (hidden_home,) = call(unpack_plain_body, [home(DV)], [y, *hidden_received])
    grads_sent = call(
        functools.partial(grads_body, n_ctx),
        [like((HEADS * CHUNK + EXTRA, WIDE), bf16)] * 4,
        [y, me, backs, kv, key_grad, value_grad, lines, cols, terms, states, payload, norm, extra],
        [VMEM((HEADS, DK, DV), bf16), VMEM((TOKENS, WIDE), bf16), VMEM((CHUNK, CHUNK), f32)],
        after=[hidden_home],
    )
    grads_received = shift_all(grads_sent)
    (query_home,) = call(unpack_plain_body, [home(DK)], [y, *query_received], cost=BIG)
    gate = like((CHUNKS * HEADS, CHUNK), bf16)
    value_home, key_home, input_home, forget_home = call(
        unpack_body, [home(DV), home(DK), gate, gate], [y, *grads_received], after=[query_home]
    )
    return (hidden_home, query_home, key_home, value_home, input_home, forget_home)


def solution(mesh):
    spec = P(None, ("ctx", "head"), None)
    flat = P(None, ("ctx", "head"))
    return jax.shard_map(
        shards,
        mesh=mesh,
        in_specs=(spec, spec, spec, flat, flat, spec, P("ctx")),
        out_specs=(spec, spec, spec, spec, flat, flat),
        check_vma=False,
    )
```

```python
import functools

import jax
import jax.numpy as jnp
from jax import lax
from jax.experimental import pallas as pl
from jax.experimental.pallas import tpu as pltpu
from jax.sharding import PartitionSpec as P

f32, bf16 = jnp.float32, jnp.bfloat16
CHUNK, CHUNKS, TOKENS = 128, 4, 512
HEADS = 2
DK, DV = 256, 512
WIDE = DK + DV
EXTRA = 16
SLICES = 32
NEG = -1e30
BIG = 10**10
SCALE = DK ** (-0.5)
ROWS = 256
VMEM = pltpu.VMEM
PARAMS = pltpu.CompilerParams(vmem_limit_bytes=28 * 1024 * 1024)


def dot(left, right, cl, cr, precision=None):
    return lax.dot_general(
        left, right, (((cl,), (cr,)), ((), ())), preferred_element_type=f32, precision=precision
    )


def exact(left, right):
    return dot(left, right, 1, 0, lax.Precision.HIGHEST)


def column(bundle, first):
    return jnp.concatenate([bundle[:, first + c : first + c + 1] for c in range(CHUNKS)], axis=0)


def line(bundle, first):
    return jnp.concatenate([bundle[first + c : first + c + 1, :] for c in range(CHUNKS)], axis=1)


def chunk_of(y, shift):
    return lax.rem(y + shift + CHUNKS, CHUNKS)


def smem():
    return pl.BlockSpec(memory_space=pltpu.SMEM)


def whole():
    return pl.BlockSpec(memory_space=VMEM)


def pieces(source, target, sem, lanes=None):
    count = HEADS if source.shape[0] == HEADS else 1
    copies = []
    for h in range(count):
        pick = (h,) if count > 1 else (slice(None),)
        at = lambda ref, cut: ref.at[pick + cut] if cut or count > 1 else ref
        cut = (slice(None),) * (len(source.shape) - 2) + (pl.ds(0, lanes),) if lanes else ()
        copies.append(pltpu.make_async_copy(at(source, cut), at(target, ()), sem.at[h]))
    return copies


class Far:
    def __init__(self, ref, held, sem, lanes):
        self.ref, self.copies = held, dict(enumerate(pieces(ref, held, sem, lanes)))
        self.shape = held.shape

    def start(self, h):
        if h in self.copies:
            self.copies[h].start()

    def finish(self):
        for h in list(self.copies):
            self.copies.pop(h).wait()

    def __getitem__(self, index):
        first = index[0] if isinstance(index, tuple) else index
        if isinstance(first, int) and self.shape[0] == HEADS:
            if first in self.copies:
                self.copies.pop(first).wait()
        else:
            self.finish()
        return self.ref[index]


class FarOut:
    def __init__(self, ref, held, sem):
        self.ref, self.copies = held, pieces(held, ref, sem)
        self.shape, self.sent = held.shape, 0

    def send(self, upto):
        while self.sent < upto:
            self.copies[self.sent].start()
            self.sent += 1

    def finish(self):
        for copy in self.copies:
            copy.wait()

    def __getitem__(self, index):
        return self.ref[index]

    def __setitem__(self, index, value):
        first = index[0] if isinstance(index, tuple) else index
        if isinstance(first, int) and len(self.copies) > 1:
            self.send(first)
        self.ref[index] = value


def call(body, outs, ins, scratch=(), cost=1, after=(), far=(), raw=(), loose=(), far_outs=(), raw_outs=()):
    far = dict(far) if isinstance(far, dict) else {i: None for i in far}
    hbm = pl.BlockSpec(memory_space=pltpu.HBM)
    free = pl.BlockSpec(memory_space=pl.ANY)
    buffers = [VMEM(ins[i].shape[:-1] + (n or ins[i].shape[-1],), ins[i].dtype) for i, n in far.items()]
    buffers += [VMEM(outs[i].shape, outs[i].dtype) for i in far_outs]

    def run(*refs):
        in_refs = list(refs[: len(ins)])
        refs = refs[len(ins) + len(after) :]
        out_refs, refs = list(refs[: len(outs)]), refs[len(outs) :]
        own, held, sems = refs[: len(scratch)], refs[len(scratch) :], refs[-1]
        for k, (i, lanes) in enumerate(far.items()):
            in_refs[i] = Far(in_refs[i], held[k], sems.at[k], lanes)
        for h in range(HEADS):
            for i in far:
                in_refs[i].start(h)
        for k, i in enumerate(far_outs, len(far)):
            out_refs[i] = FarOut(out_refs[i], held[k], sems.at[k])
        body(*in_refs, *out_refs, *own)
        for i in far_outs:
            out_refs[i].send(len(out_refs[i].copies))
        for i in far:
            in_refs[i].finish()
        for i in far_outs:
            out_refs[i].finish()

    def place(i, a):
        if a.dtype == jnp.int32 and a.size <= 2:
            return smem()
        return free if i in loose else hbm if i in far or i in raw else whole()

    def pin(i, a):
        held = (i in far or i in raw) and i not in loose
        return pltpu.with_memory_space_constraint(a, pltpu.HBM) if held else a

    far_all = set(far_outs) | set(raw_outs)
    return pl.pallas_call(
        run,
        out_shape=[pltpu.HBM(o.shape, o.dtype) if i in far_all else o for i, o in enumerate(outs)],
        in_specs=[place(i, a) for i, a in enumerate(ins)] + [hbm if a.ndim == 3 else free for a in after],
        out_specs=tuple(hbm if i in far_all else whole() for i in range(len(outs))),
        scratch_shapes=[*scratch, *buffers, pltpu.SemaphoreType.DMA((max(1, len(buffers)), HEADS))],
        compiler_params=PARAMS,
        cost_estimate=pl.CostEstimate(flops=cost, bytes_accessed=cost, transcendentals=0),
    )(*[pin(i, a) for i, a in enumerate(ins)], *(pltpu.with_memory_space_constraint(a, pltpu.HBM) if a.ndim == 3 else a for a in after))


def like(shape, dtype):
    return jax.ShapeDtypeStruct(shape, dtype)


def run_copies(pairs, sems):
    copies = [pltpu.make_async_copy(a, b, sems.at[k]) for k, (a, b) in enumerate(pairs)]
    for copy in copies:
        copy.start()
    return copies


def pack_body(gates, y_ref, a_ref, b_ref, *rest):
    *rest, sems = rest
    outs = rest[-CHUNKS:]
    pairs = []
    for shift in (1, 3, 2, 0):
        dest = chunk_of(y_ref[0], shift)
        for h in range(HEADS):
            rows = pl.ds(h * CHUNK, CHUNK)
            pairs.append((a_ref.at[dest * HEADS + h], outs[shift].at[rows, pl.ds(0, DK)]))
            pairs.append((b_ref.at[dest * HEADS + h], outs[shift].at[rows, pl.ds(DK, DV)]))
    copies = run_copies(pairs, sems)
    if gates:
        both = jnp.concatenate([rest[0][...].astype(f32), rest[1][...].astype(f32)], axis=0)
        for out in outs:
            out[HEADS * CHUNK : HEADS * CHUNK + EXTRA, 0:CHUNK] = both.astype(bf16)
    for copy in copies:
        copy.wait()


def pack(y, narrow, wide, gates=(), after=()):
    rows = HEADS * CHUNK + (EXTRA if gates else 0)
    return call(
        functools.partial(pack_body, bool(gates)),
        [like((rows, WIDE), bf16)] * CHUNKS,
        [y, narrow, wide, *gates],
        [pltpu.SemaphoreType.DMA((4 * CHUNKS,))],
        after=after,
        far=(3, 4) if gates else (),
        raw=(1, 2),
    )


def assemble(all_ref, y, received):
    for h in range(HEADS):
        for shift, ref in enumerate(received):
            all_ref[h, chunk_of(y, -shift)] = ref[h * CHUNK : (h + 1) * CHUNK, :]


def update_body(
    y_ref, kv0, kv1, kv2, kv3, doc_ref, all_ref, line_ref, col_ref, pay_ref, gates, lines, extra
):
    y = y_ref[0]
    received = (kv0, kv1, kv2, kv3)
    assemble(all_ref, y, received)
    for shift, ref in enumerate(received):
        gates[chunk_of(y, -shift)] = ref[HEADS * CHUNK : HEADS * CHUNK + EXTRA, 0:CHUNK].astype(f32)
    row = lax.broadcasted_iota(jnp.int32, (16, CHUNK), 0)
    for c in range(CHUNKS):
        tile = gates[c]
        for h in range(HEADS):
            pick = y * HEADS + h
            lines[1, h * CHUNKS + c : h * CHUNKS + c + 1, :] = jnp.sum(
                jnp.where(row == pick, tile, 0.0), axis=0, keepdims=True
            )
            lines[0, h * CHUNKS + c : h * CHUNKS + c + 1, :] = jnp.sum(
                jnp.where(row == pick + 8, tile, 0.0), axis=0, keepdims=True
            )
    forget = lines[0, 0:8]
    fade = jnp.exp(-forget)
    lines[0, 0:8] = -jnp.log1p(fade)
    lines[0, 8:12] = doc_ref[...].astype(f32)
    lines[0, 12:16] = jnp.zeros((4, CHUNK), f32)
    closed = fade / (1.0 + fade)
    before = lax.broadcasted_iota(jnp.int32, (CHUNK, CHUNK), 0)
    after = lax.broadcasted_iota(jnp.int32, (CHUNK, CHUNK), 1)
    total = exact(lines[0], (before <= after).astype(f32))
    whole_lines = []
    for group in range(3):
        run = jnp.zeros((1, 1), f32)
        for c in range(CHUNKS):
            here = total[group * CHUNKS + c : group * CHUNKS + c + 1, :]
            whole_lines.append(here + run)
            run = run + here[:, CHUNK - 1 : CHUNK]
    segment = jnp.concatenate(whole_lines[8:12], axis=0)
    segment_end = segment[3:4, CHUNK - 1 : CHUNK]
    extra[...] = jnp.zeros_like(extra)
    for h in range(HEADS):
        cumulative = jnp.concatenate(whole_lines[h * CHUNKS : (h + 1) * CHUNKS], axis=0)
        end = cumulative[3:4, CHUNK - 1 : CHUNK]
        ingate = lines[1, h * CHUNKS : (h + 1) * CHUNKS]
        line_ref[h] = jnp.zeros((CHUNK, CHUNK), f32)
        line_ref[h, 0:4] = cumulative
        line_ref[h, 4:8] = ingate - cumulative
        line_ref[h, 8:12] = jnp.where(segment == segment_end, jnp.exp(end - cumulative + ingate), 0.0)
        line_ref[h, 12:16] = jnp.where(segment == 0.0, jnp.exp(cumulative), 0.0)
        line_ref[h, 16:20] = segment
        line_ref[h, 20:24] = closed[h * CHUNKS : (h + 1) * CHUNKS]
        col_ref[h] = line_ref[h].T
        decay = jnp.where(segment_end == 0.0, jnp.exp(end), 0.0)
        keys = all_ref[h, :, :, 0:DK].reshape(TOKENS, DK)
        values = all_ref[h, :, :, DK:WIDE].reshape(TOKENS, DV)
        keys_alpha = (column(col_ref[h], 8) * keys.astype(f32)).astype(bf16)
        update = dot(keys_alpha, values, 0, 0).astype(bf16)
        scatter(pay_ref, update, h)
        update_n = jnp.sum(keys_alpha.astype(f32), axis=0, keepdims=True)
        for half in range(2):
            extra[2 * h + half : 2 * h + half + 1, :] = update_n[:, half * CHUNK : (half + 1) * CHUNK]
            extra[4 + 2 * h + half : 5 + 2 * h + half, :] = jnp.broadcast_to(decay, (1, CHUNK))
    share(pay_ref, extra[...])


def share(pay_ref, lines):
    high = lines.astype(bf16).astype(f32)
    tile = jnp.concatenate([high, lines - high], axis=0).astype(bf16)
    for i in range(SLICES):
        pay_ref[i, :, 2 * DK : 2 * DK + CHUNK] = tile


def shared(pay_ref, index):
    tile = pay_ref[index, :, 2 * DK : 2 * DK + CHUNK].astype(f32)
    return tile[0:8] + tile[8:16]


def scatter(pay_ref, matrix, h, first=0):
    for i in range(SLICES):
        r, c = i // 2, i % 2
        here = slice(first + h * DK, first + (h + 1) * DK)
        pay_ref[i, :, here] = matrix[16 * r : 16 * (r + 1), DK * c : DK * (c + 1)]


def collect(matrix_ref, pay_ref, h):
    for i in range(SLICES):
        r, c = i // 2, i % 2
        matrix_ref[h, 16 * r : 16 * (r + 1), DK * c : DK * (c + 1)] = pay_ref[i, :, h * DK : (h + 1) * DK]


def pair_body(y_ref, qg0, qg1, qg2, qg3, kv_ref, line_ref, col_ref, all_ref, pair_ref, weight_ref, sum_ref):
    assemble(all_ref, y_ref[0], (qg0, qg1, qg2, qg3))
    for h in range(HEADS):
        sum_ref[h] = jnp.zeros((CHUNK, CHUNK), f32)
        keys = kv_ref[h, :, :, 0:DK].reshape(TOKENS, DK)
        query = all_ref[h, :, :, 0:DK].reshape(TOKENS, DK)
        for r in range(TOKENS // ROWS):
            last = (r + 1) * ROWS
            here = slice(r * ROWS, last)
            scores = dot(query[here], keys[0:last], 1, 1) * SCALE
            weight = weights(line_ref, col_ref, h, r)
            weight_ref[h, here, 0:last] = weight.astype(bf16)
            pair = (weight * scores).astype(bf16)
            pair_ref[h, here, 0:last] = pair
            put_column(sum_ref, h, 0, jnp.sum(pair.astype(f32), axis=1, keepdims=True), r)


def weights(line_ref, col_ref, h, r):
    last = (r + 1) * ROWS
    here = slice(r * ROWS, last)
    position = lax.broadcasted_iota(jnp.int32, (ROWS, last), 0) + r * ROWS
    source = lax.broadcasted_iota(jnp.int32, (ROWS, last), 1)
    log_weight = column(col_ref[h], 0)[here] + line(line_ref[h], 4)[:, 0:last]
    allowed = (position >= source) & (column(col_ref[h], 16)[here] == line(line_ref[h], 16)[:, 0:last])
    return jnp.exp(jnp.where(allowed, log_weight, NEG))


def put_column(ref, h, first, value, r=0):
    first += r * (ROWS // CHUNK)
    for c in range(value.shape[0] // CHUNK):
        ref[h, :, first + c : first + c + 1] = value[c * CHUNK : (c + 1) * CHUNK]


def norm_line(norm_ref, h):
    both = [norm_ref[2 * h + half : 2 * h + half + 1, :] for half in range(2)]
    return jnp.concatenate(both, axis=1).astype(bf16).astype(f32)


def spread(extra):
    return jnp.concatenate([extra[4 + r : 5 + r, :] for r in range(4)], axis=1)


def adjoint_body(n_ctx, me_ref, in_ref, qg_ref, col_ref, sum_ref, pay_ref, norm_ref, extra_ref, num_ref, cols_ref):
    mine = SLICES // n_ctx
    me = me_ref[0]
    norm = jnp.zeros((4, CHUNK), f32)
    for j in range(n_ctx):
        extra = shared(in_ref, j * mine)
        extra_ref[j] = extra
        norm = jnp.where(j < me, extra[4:8] * norm + extra[0:4], norm)
    norm_ref[...] = jnp.concatenate([norm, jnp.zeros((4, CHUNK), f32)], axis=0)
    for h in range(HEADS):
        cols_ref[h] = jnp.zeros((CHUNK, CHUNK), f32)
        query = qg_ref[h, :, :, 0:DK].reshape(TOKENS, DK).astype(f32)
        beta = column(col_ref[h], 12)
        cross = jnp.sum(query * norm_line(norm_ref, h), axis=1, keepdims=True)
        denominator = column(sum_ref[h], 0) + beta * cross * SCALE
        norm = jnp.sqrt(denominator * denominator + 1.0)
        put_column(cols_ref, h, 0, denominator)
        put_column(cols_ref, h, 4, norm)
        grad = qg_ref[h, :, :, DK:WIDE].reshape(TOKENS, DV).astype(f32)
        num_grad = (grad / norm).astype(bf16)
        num_ref[h] = num_grad
        query_beta = (beta * query * SCALE).astype(bf16)
        scatter(pay_ref, dot(query_beta, num_grad, 0, 0).astype(bf16), h, 2 * DK)
    state = jnp.zeros((mine, 16, 2 * DK), f32)
    for j in range(n_ctx):
        here = slice(j * mine, (j + 1) * mine)
        pay_ref[here, :, 0 : 2 * DK] = state.astype(bf16)
        state = spread(extra_ref[j]) * state + in_ref[here, :, 0 : 2 * DK].astype(f32)


def local_body(kv_ref, pair_ref, num_ref, weight_ref, inner_ref, score_ref, value_ref):
    for h in range(HEADS):
        values = kv_ref[h, :, :, DK:WIDE].reshape(TOKENS, DV)
        for r in range(TOKENS // ROWS):
            last = (r + 1) * ROWS
            here = slice(r * ROWS, last)
            inner_ref[h, here] = dot(pair_ref[h, here, 0:last], values[0:last], 1, 0).astype(bf16)
            inner = dot(num_ref[h, here], values[0:last], 1, 1)
            score_ref[h, here, 0:last] = (weight_ref[h, here, 0:last].astype(f32) * inner).astype(bf16)
        for s in range(TOKENS // ROWS):
            first = s * ROWS
            here = slice(first, first + ROWS)
            inner = dot(pair_ref[h, first:TOKENS, here], num_ref[h, first:TOKENS], 0, 0)
            value_ref[h, here] = inner.astype(bf16)


def hidden_body(
    n_ctx, y_ref, in_ref, extra_ref, qg_ref, inner_ref, col_ref, cols_ref, o0, o1, o2, o3, pay_ref, state_ref, den_ref, done, lines
):
    mine = SLICES // n_ctx
    lines[...] = jnp.zeros_like(lines)
    for h in range(HEADS):
        collect(state_ref, in_ref, h)
        state = state_ref[h]
        den_ref[h] = jnp.zeros((CHUNK, CHUNK), f32)
        beta = column(col_ref[h], 12) * SCALE
        denominator = column(cols_ref[h], 0)
        inverse = 1.0 / column(cols_ref[h], 4)
        factor = -denominator * inverse * inverse
        for r in range(TOKENS // ROWS):
            here = slice(r * ROWS, (r + 1) * ROWS)
            chunks = slice(r * ROWS // CHUNK, (r + 1) * ROWS // CHUNK)
            query = qg_ref[h, chunks, :, 0:DK].reshape(ROWS, DK)
            grad = qg_ref[h, chunks, :, DK:WIDE].reshape(ROWS, DV)
            cross = beta[here] * dot(query, state, 1, 0)
            hidden = (inner_ref[h, here].astype(f32) + cross) * inverse[here]
            done[here, :] = hidden.astype(bf16)
            product = jnp.sum(grad.astype(f32) * hidden, axis=1, keepdims=True)
            den_grad = product * factor[here]
            put_column(den_ref, h, 0, den_grad, r)
            query_beta = (beta[here] * query.astype(f32)).astype(bf16).astype(f32)
            total = jnp.sum(query_beta * den_grad, axis=0, keepdims=True)
            for half in range(2):
                lines[2 * h + half : 2 * h + half + 1, :] += total[:, half * CHUNK : (half + 1) * CHUNK]
        send(done, y_ref[0], h, (o0, o1, o2, o3))
    share(pay_ref, lines[...])
    back = jnp.zeros((mine, 16, 2 * DK), f32)
    for j in reversed(range(n_ctx)):
        here = slice(j * mine, (j + 1) * mine)
        pay_ref[here, :, 0 : 2 * DK] = back.astype(bf16)
        back = spread(extra_ref[j]) * back + in_ref[here, :, 2 * DK : 4 * DK].astype(f32)


def send(done, y, h, outs):
    for shift, out in enumerate(outs):
        first = pl.multiple_of(chunk_of(y, shift) * CHUNK, CHUNK)
        out[h * CHUNK : (h + 1) * CHUNK, :] = done[pl.ds(first, CHUNK), :]


def score_body(
    y_ref, kv_ref, qg_ref, num_ref, weight_ref, inner_ref, state_ref, norm_ref, col_ref, den_ref, o0, o1, o2, o3, terms_ref, key_ref, score, done
):
    for h in range(HEADS):
        terms_ref[h] = jnp.zeros((CHUNK, CHUNK), f32)
        keys = kv_ref[h, :, :, 0:DK].reshape(TOKENS, DK)
        query = qg_ref[h, :, :, 0:DK].reshape(TOKENS, DK)
        beta = column(col_ref[h], 12) * SCALE
        den_grad = column(den_ref[h], 0)
        norm_bf = norm_line(norm_ref, h)
        state = state_ref[h]
        for r in range(TOKENS // ROWS):
            last = (r + 1) * ROWS
            here = slice(r * ROWS, last)
            weight = weight_ref[h, here, 0:last].astype(f32)
            inner = inner_ref[h, here, 0:last].astype(f32)
            score[here, 0:last] = (inner + weight * den_grad[here]).astype(bf16)
            from_state = dot(num_ref[h, here], state, 1, 1) + den_grad[here] * norm_bf
            query_grad = dot(score[here, 0:last], keys[0:last], 1, 0) * SCALE + beta[here] * from_state
            done[here, :] = query_grad.astype(bf16)
            term = jnp.sum(query[here].astype(f32) * query_grad, axis=1, keepdims=True)
            put_column(terms_ref, h, 0, term, r)
        send(done, y_ref[0], h, (o0, o1, o2, o3))
        for s in range(TOKENS // ROWS):
            first = s * ROWS
            here = slice(first, first + ROWS)
            inner = dot(score[first:TOKENS, here], query[first:TOKENS], 0, 0) * SCALE
            key_ref[h, here] = inner.astype(bf16)


def grads_body(
    n_ctx, y_ref, me_ref, in_ref, kv_ref, key_ref, value_ref, line_ref, col_ref, terms_ref, state_ref, pay_ref, norm_ref, extra_ref, o0, o1, o2, o3, back, done, cols
):
    mine = SLICES // n_ctx
    y, me = y_ref[0], me_ref[0]
    norm = jnp.zeros((4, CHUNK), f32)
    for j in reversed(range(n_ctx)):
        norm = jnp.where(j > me, extra_ref[j][4:8] * norm + shared(in_ref, j * mine)[0:4], norm)
    back_n = norm.astype(bf16).astype(f32)
    extra = extra_ref[me]
    state_n = norm_ref[0:4, :].astype(bf16).astype(f32)
    later_n = (extra[4:8] * state_n + extra[0:4]) * back_n
    decay = spread(extra)
    later = jnp.zeros((16, 2 * DK), f32)
    for i in range(SLICES):
        state = decay * state_ref[i, :, 0 : 2 * DK].astype(f32) + pay_ref[i, :, 0 : 2 * DK].astype(f32)
        later = later + state * in_ref[i, :, 0 : 2 * DK].astype(f32)
    cols[...] = jnp.zeros_like(cols)
    for h in range(HEADS):
        collect(back, in_ref, h)
        back_bf = back[h]
        keys = kv_ref[h, :, :, 0:DK].reshape(TOKENS, DK)
        values = kv_ref[h, :, :, DK:WIDE].reshape(TOKENS, DV)
        alpha = column(col_ref[h], 8)
        row = jnp.concatenate([back_n[2 * h : 2 * h + 1], back_n[2 * h + 1 : 2 * h + 2]], axis=1)
        for r in range(TOKENS // ROWS):
            here = slice(r * ROWS, (r + 1) * ROWS)
            key_grad = key_ref[h, here].astype(f32) + alpha[here] * (dot(values[here], back_bf, 1, 1) + row)
            value_grad = value_ref[h, here].astype(f32) + alpha[here] * dot(keys[here], back_bf, 1, 0)
            done[here, 0:DV] = value_grad.astype(bf16)
            done[here, DV : DV + DK] = key_grad.astype(bf16)
            key_term = jnp.sum(keys[here].astype(f32) * key_grad, axis=1, keepdims=True)
            for c in range(ROWS // CHUNK):
                piece = key_term[c * CHUNK : (c + 1) * CHUNK]
                k = r * (ROWS // CHUNK) + c
                cols[:, h * 4 + k : h * 4 + k + 1] = terms_ref[h, :, k : k + 1] - piece
                cols[:, 8 + h * 4 + k : 9 + h * 4 + k] = piece
        send(done, y, h, (o0, o1, o2, o3))
    lines = cols[...].T[0:16]
    before = lax.broadcasted_iota(jnp.int32, (CHUNK, CHUNK), 0)
    after = lax.broadcasted_iota(jnp.int32, (CHUNK, CHUNK), 1)
    suffix = exact(lines, (before >= after).astype(f32))
    tiles = [[None] * HEADS for _ in range(CHUNKS)]
    for h in range(HEADS):
        run = jnp.sum(later[:, h * DK : (h + 1) * DK], keepdims=True) + jnp.sum(
            later_n[2 * h : 2 * h + 2], keepdims=True
        )
        for c in reversed(range(CHUNKS)):
            here = suffix[h * 4 + c : h * 4 + c + 1]
            tiles[c][h] = (here + run) * line_ref[h, 20 + c : 21 + c]
            run = run + here[:, 0:1]
    for c in range(CHUNKS):
        rows = [lines[8 + h * 4 + c : 9 + h * 4 + c] for h in range(HEADS)] + tiles[c]
        cols[c * 16 : (c + 1) * 16, :] = jnp.concatenate(rows + [jnp.zeros((12, CHUNK), f32)], axis=0)
    for shift, out in enumerate((o0, o1, o2, o3)):
        first = pl.multiple_of(chunk_of(y, shift) * 16, 16)
        out[HEADS * CHUNK : HEADS * CHUNK + EXTRA, 0:CHUNK] = cols[pl.ds(first, 16), :].astype(bf16)


def unpack_plain_body(y_ref, r0, r1, r2, r3, out_ref, sems):
    pairs = []
    for shift, ref in ((1, r1), (2, r2), (3, r3), (0, r0)):
        source = chunk_of(y_ref[0], -shift)
        if shift == 0:
            copies = run_copies(pairs, sems)
            r0.finish()
            pairs, ref = [], r0.ref
        for h in range(HEADS):
            pairs.append((ref.at[pl.ds(h * CHUNK, CHUNK), :], out_ref.at[source * HEADS + h]))
    for copy in copies + run_copies(pairs, sems.at[pl.ds(6, 2)]):
        copy.wait()


def unpack_body(y_ref, r0, r1, r2, r3, wide_ref, narrow_ref, input_ref, forget_ref, tiles, sems):
    y = y_ref[0]
    pairs = []
    for shift, ref in enumerate((r0, r1, r2, r3)):
        pairs.append((ref.at[pl.ds(HEADS * CHUNK, EXTRA), pl.ds(0, CHUNK)], tiles.at[shift]))
    for shift, ref in enumerate((r0, r1, r2, r3)):
        source = chunk_of(y, -shift)
        for h in range(HEADS):
            rows = pl.ds(h * CHUNK, CHUNK)
            pairs.append((ref.at[rows, pl.ds(0, DV)], wide_ref.at[source * HEADS + h]))
            pairs.append((ref.at[rows, pl.ds(DV, DK)], narrow_ref.at[source * HEADS + h]))
    copies = run_copies(pairs, sems)
    row = lax.broadcasted_iota(jnp.int32, (8, CHUNK), 0)
    sums = [jnp.zeros((8, CHUNK), f32)] * 2
    for shift in range(CHUNKS):
        copies[shift].wait()
        tile = tiles[shift].astype(f32)
        for h in range(HEADS):
            for k in range(2):
                here = row == chunk_of(y, -shift) * HEADS + h
                sums[k] = sums[k] + jnp.where(here, tile[2 * k + h : 2 * k + h + 1], 0.0)
    input_ref[...] = sums[0].astype(bf16)
    forget_ref[...] = sums[1].astype(bf16)
    for copy in copies[CHUNKS:]:
        copy.wait()


def shift_all(parts):
    moved = [parts[0]]
    for shift, part in enumerate(parts[1:], 1):
        pairs = [(i, (i + shift) % CHUNKS) for i in range(CHUNKS)]
        moved.append(lax.ppermute(part, "head", pairs))
    return moved


def home(width):
    return like((CHUNKS * HEADS, CHUNK, width), bf16)


def unpack(y, received, width, cost=1):
    return call(
        unpack_plain_body,
        [home(width)],
        [y, *received],
        [pltpu.SemaphoreType.DMA((2 * CHUNKS,))],
        cost=cost,
        far=(1,),
        raw=(2, 3, 4),
        loose=(2, 3, 4),
        raw_outs=(0,),
    )


def exchange(part):
    return lax.all_to_all(part, "ctx", split_axis=0, concat_axis=0, tiled=True)


def shards(query, keys, values, igate, fgate, hidden_output_gradient, doc_start):
    n_ctx = lax.axis_size("ctx")
    y = lax.axis_index("head").astype(jnp.int32).reshape(1)
    me = lax.axis_index("ctx").astype(jnp.int32).reshape(1)
    kv_received = shift_all(pack(y, keys, values, (igate, fgate)))
    qg_received = shift_all(pack(y, query, hidden_output_gradient, after=[kv_received[1]]))
    tokens = like((HEADS, CHUNKS, CHUNK, WIDE), bf16)
    bundle = like((HEADS, CHUNK, CHUNK), f32)
    square_bf = like((HEADS, TOKENS, TOKENS), bf16)
    carried = like((SLICES, 16, 2 * DK + CHUNK), bf16)
    kv, lines, cols, payload = call(
        update_body,
        [tokens, bundle, bundle, carried],
        [y, *kv_received, doc_start.reshape(CHUNKS, CHUNK)],
        [VMEM((CHUNKS, 16, CHUNK), f32), VMEM((2, 16, CHUNK), f32), VMEM((8, CHUNK), f32)],
        far=(5,),
        far_outs=(0, 3),
    )
    updates = exchange(payload)
    qg, pair, weight, sums = call(
        pair_body,
        [tokens, square_bf, square_bf, bundle],
        [y, *qg_received, kv, lines, cols],
        cost=BIG,
        far={5: DK, 1: None, 2: None, 3: None, 4: None},
        loose=(1, 2, 3, 4),
        far_outs=(1, 2, 3),
    )
    both, norm, extra, num_grad, norm_cols = call(
        functools.partial(adjoint_body, n_ctx),
        [
            like((SLICES, 16, 4 * DK), bf16),
            like((8, CHUNK), f32),
            like((n_ctx, 8, CHUNK), f32),
            like((HEADS, TOKENS, DV), bf16),
            bundle,
        ],
        [me, updates, qg, cols, sums],
        far=(1, 4),
        loose=(1,),
        far_outs=(0, 3, 4),
    )
    states = exchange(both)
    wide = like((HEADS, TOKENS, DV), bf16)
    inner, inner_score, value_grad = call(
        local_body,
        [wide, square_bf, wide],
        [kv, pair, num_grad, weight],
        cost=BIG,
        far=(0, 1, 2, 3),
        far_outs=(0, 1, 2),
    )
    hidden_part = like((HEADS * CHUNK, DV), bf16)
    *hidden_sent, back_part, state, den_grad = call(
        functools.partial(hidden_body, n_ctx),
        [hidden_part] * 4 + [carried, like((HEADS, DK, DV), bf16), bundle],
        [y, states, extra, qg, inner, cols, norm_cols],
        [VMEM((TOKENS, DV), bf16), VMEM((8, CHUNK), f32)],
        far=(1, 6, 4),
        loose=(1,),
        far_outs=(0, 1, 2, 3, 4, 5, 6),
    )
    backs = exchange(back_part)
    hidden_received = shift_all(hidden_sent)
    *query_sent, terms, key_grad = call(
        score_body,
        [like((HEADS * CHUNK, DK), bf16)] * 4 + [bundle, like((HEADS, TOKENS, DK), bf16)],
        [y, kv, qg, num_grad, weight, inner_score, state, norm, cols, den_grad],
        [VMEM((TOKENS, TOKENS), bf16), VMEM((TOKENS, DK), bf16)],
        cost=BIG,
        far={9: None, 5: None, 4: None, 3: None, 6: None, 1: DK},
        far_outs=(0, 1, 2, 3, 4, 5),
    )
    query_received = shift_all(query_sent)
    (hidden_home,) = unpack(y, hidden_received, DV)
    grads_sent = call(
        functools.partial(grads_body, n_ctx),
        [like((HEADS * CHUNK + EXTRA, WIDE), bf16)] * 4,
        [y, me, backs, kv, key_grad, value_grad, lines, cols, terms, states, payload, norm, extra],
        [VMEM((HEADS, DK, DV), bf16), VMEM((TOKENS, WIDE), bf16), VMEM((CHUNK, CHUNK), f32)],
        after=[hidden_home],
        far={2: None, 3: None, 4: None, 5: None, 8: None, 9: 2 * DK, 10: 2 * DK},
        loose=(2, 9),
    )
    grads_received = shift_all(grads_sent)
    (query_home,) = unpack(y, query_received, DK, BIG)
    gate = like((CHUNKS * HEADS, CHUNK), bf16)
    value_home, key_home, input_home, forget_home = call(
        unpack_body,
        [home(DV), home(DK), gate, gate],
        [y, *grads_received],
        [VMEM((CHUNKS, EXTRA, CHUNK), bf16), pltpu.SemaphoreType.DMA((5 * CHUNKS,))],
        after=[query_home],
        raw=(1, 2, 3, 4),
        loose=(1, 2, 3, 4),
        raw_outs=(0, 1),
    )
    return (hidden_home, query_home, key_home, value_home, input_home, forget_home)


def solution(mesh):
    spec = P(None, ("ctx", "head"), None)
    flat = P(None, ("ctx", "head"))
    return jax.shard_map(
        shards,
        mesh=mesh,
        in_specs=(spec, spec, spec, flat, flat, spec, P("ctx")),
        out_specs=(spec, spec, spec, spec, flat, flat),
        check_vma=False,
    )
```
